128 devices in a mesh: gx: 16 (over z_lo, x, core), gy: 8 (over z_hi, y).
Axes of the slice: x: 4, y: 4, z: 4 (z_hi: 2, z_lo: 2; z = z_hi * 2 + z_lo), core: 2. Of those that a mesh axis runs over, the one named last changes fastest.
Arguments:
- directions: float32 [64, 6, 128, 1024], P(None, None, 'gx', 'gy'), may hold values from -6 to 6
- node_scale: float32 [128, 1024], P('gx', 'gy'), may hold values from 0.5 to 1.5
- boundary_mask: int32 [128, 1024], P('gx', 'gy'), may hold values 0 or 1
- stiffener_rows: int32 [8], replicated, may hold values from 0 to 127
- stiffener_cols: int32 [16], replicated, may hold values from 0 to 1023
- center_stiffness: float32 [6], replicated, may hold values from 3 to 6
- couplings: float32 [6, 6, 6], replicated, may hold values from -0.04 to 0.04
- stiffener_stiffness: float32 [2, 6], replicated, may hold values from 0.5 to 4
Outputs:
- basis: float32 [64, 6, 128, 1024], P(None, None, 'gx', 'gy')
- projected: float32 [64, 64], replicated
The draws below stay inside these ranges and needn't reach their ends.
All inputs are finite; a program needn't handle non-finite values. No bound on the sum of `boundary_mask` on one device may be relied on, other than what follows from the above.
Results may differ from the reference program's by a relative error of at most 0.00016.
Values sent between devices are 32-bit elements; how exact they have to be, the bound alone decides.
A program may use at most 192 MiB of HBM per device.

```python
import math
import jax
import jax.numpy as jnp
from jax import lax

K = 64
FRAMES = 8
STRINGERS = 16
NX = 128
NY = 1024


def set_ends(values, rng, least, top_value):
    longest = values.shape.index(max(values.shape))
    spots = []
    for shift in (0, 1):
        where = [jax.random.randint(jax.random.fold_in(rng, axis), (), 0, length) for axis, length in enumerate(values.shape)]
        where[longest] = (where[longest] + shift) % values.shape[longest]
        spots.append(tuple(where))
    return values.at[spots[0]].set(least).at[spots[1]].set(top_value)


def block_levels(rng, shape, cuts, smallest, top_value):
    gain, own = 1.0, jax.random.fold_in(rng, 6)
    for position, blocks in cuts:
        heights = jnp.exp(jax.random.uniform(jax.random.fold_in(own, position), (blocks,), jnp.float32, smallest / len(cuts), top_value / len(cuts)))
        gain = gain * jnp.repeat(heights, shape[position] // blocks).reshape([-1 if axis == position else 1 for axis in range(len(shape))])
    return gain


def noise(key, dims, scale, most, split=(), kind=jnp.bfloat16):
    level = block_levels(key, dims, split, -0.22, 0.18) if split else 1.0
    drawn = jax.random.normal(key, dims, jnp.float32) * scale * level
    return jnp.minimum(jnp.maximum(drawn, -most), most).astype(kind)


def setup_inputs(seed: int = 0) -> dict:
    splits = jax.random.split(jax.random.key(seed), 9)
    return {
        "directions": noise(splits[0], (K, 6, NX, NY), 1.0, 6.0, ((2, 16), (3, 8)), jnp.float32),
        "node_scale": jnp.clip(jnp.exp(math.log(1.5) - 1.0986123 * jax.random.uniform(splits[1], (NX, NY), jnp.float32) ** block_levels(splits[1], (NX, NY), ((0, 16), (1, 8)), -0.2, 0.2)), 0.5, 1.5),
        "boundary_mask": set_ends((jax.random.randint(splits[2], (NX, NY), 0, 8) < 1).astype(jnp.int32), jax.random.fold_in(splits[2], 1), 0, 1),
        "stiffener_rows": set_ends(jax.random.randint(splits[3], (FRAMES,), 0, NX), jax.random.fold_in(splits[3], 1), 0, NX - 1).astype(jnp.int32),
        "stiffener_cols": set_ends(jax.random.randint(splits[4], (STRINGERS,), 0, NY), jax.random.fold_in(splits[4], 1), 0, NY - 1).astype(jnp.int32),
        "center_stiffness": jnp.clip(jax.random.uniform(splits[5], (6,), jnp.float32, 3.0, 6.0), 3.0, 6.0),
        "couplings": jnp.clip(jax.random.uniform(splits[6], (6, 6, 6), jnp.float32, -0.04, 0.04), -0.04, 0.04),
        "stiffener_stiffness": jnp.clip(jnp.exp(jax.random.uniform(splits[7], (2, 6), jnp.float32, math.log(0.5), math.log(4.0))), 0.5, 4.0),
    }


OFFSETS = ((1, 0), (0, 1), (1, 1), (1, -1), (2, 0), (0, 2))

def couple(padded, scaled, center_stiffness, couplings, stiffener_stiffness, rows_hit, cols_hit):
    extent_x = scaled.shape[2]
    extent_y = scaled.shape[3]

    def window(step_x, step_y):
        return padded[:, :, 2 + step_x:2 + step_x + extent_x, 2 + step_y:2 + step_y + extent_y]
    total = center_stiffness[None, :, None, None] * scaled
    for offset_index, (step_x, step_y) in enumerate(OFFSETS):
        block = couplings[offset_index]
        total = total + jnp.einsum('cd,kdxy->kcxy', block, window(step_x, step_y), precision=lax.Precision.HIGHEST)
        total = total + jnp.einsum('dc,kdxy->kcxy', block, window(-step_x, -step_y), precision=lax.Precision.HIGHEST)
    along_y = 2.0 * scaled - window(0, 1) - window(0, -1)
    along_x = 2.0 * scaled - window(1, 0) - window(-1, 0)
    total = total + stiffener_stiffness[0][None, :, None, None] * rows_hit[None, None, :, None] * along_y
    total = total + stiffener_stiffness[1][None, :, None, None] * cols_hit[None, None, None, :] * along_x
    return total

def lower_cholesky(gram):
    order = gram.shape[0]
    slots = jnp.arange(order, dtype=jnp.int32)

    def column_step(column, lower):
        pick = (slots == column).astype(gram.dtype)
        target = jnp.dot(gram, pick, precision=lax.Precision.HIGHEST)
        row_of = jnp.dot(pick, lower, precision=lax.Precision.HIGHEST)
        residue = target - jnp.dot(lower, row_of, precision=lax.Precision.HIGHEST)
        pivot = jnp.sqrt(jnp.sum(residue * pick))
        keep = (slots >= column).astype(gram.dtype)
        fresh = residue * keep / pivot
        return lower + fresh[:, None] * pick[None, :]
    return lax.fori_loop(0, order, column_step, jnp.zeros_like(gram))

def lower_inverse(lower):
    order = lower.shape[0]
    slots = jnp.arange(order, dtype=jnp.int32)

    def row_step(row, solved):
        pick = (slots == row).astype(lower.dtype)
        row_of = jnp.dot(pick, lower, precision=lax.Precision.HIGHEST)
        pivot = jnp.sum(row_of * pick)
        fresh = (pick - jnp.dot(row_of, solved, precision=lax.Precision.HIGHEST)) / pivot
        return solved + pick[:, None] * fresh[None, :]
    return lax.fori_loop(0, order, row_step, jnp.zeros_like(lower))

def reference(directions, node_scale, boundary_mask, stiffener_rows, stiffener_cols, center_stiffness, couplings, stiffener_stiffness):
    mask_value = boundary_mask.astype(jnp.float32)
    weight = node_scale * (1.0 - mask_value)
    rows_hit = lax.optimization_barrier(jnp.sum((jnp.arange(NX, dtype=jnp.int32)[:, None] == stiffener_rows[None, :]).astype(jnp.float32), axis=1))
    cols_hit = lax.optimization_barrier(jnp.sum((jnp.arange(NY, dtype=jnp.int32)[:, None] == stiffener_cols[None, :]).astype(jnp.float32), axis=1))

    def operate(field):
        scaled = weight[None, None] * field
        padded = jnp.pad(scaled, ((0, 0), (0, 0), (2, 2), (2, 2)))
        applied = couple(padded, scaled, center_stiffness, couplings, stiffener_stiffness, rows_hit, cols_hit)
        return weight[None, None] * applied + mask_value[None, None] * field
    groups = K // 8
    product = lax.map(operate, directions.reshape(groups, 8, 6, NX, NY)).reshape(K, 6, NX, NY)
    flat = product.reshape(K, -1)
    gram = jnp.dot(flat, flat.T, precision=lax.Precision.HIGHEST)
    lower = lower_cholesky(gram)
    inverse = lower_inverse(lower).T

    def cross_block(group):
        image = operate(group)
        return jnp.dot(flat, image.reshape(8, -1).T, precision=lax.Precision.HIGHEST)
    pieces = lax.map(cross_block, product.reshape(groups, 8, 6, NX, NY))
    cross = jnp.transpose(pieces, (1, 0, 2)).reshape(K, K)
    left = jnp.dot(inverse.T, cross, precision=lax.Precision.HIGHEST)
    projected = jnp.dot(left, inverse, precision=lax.Precision.HIGHEST)
    basis = math.sqrt(6.0 * NX * NY) * jnp.dot(inverse.T, flat, precision=lax.Precision.HIGHEST)
    return (basis.reshape(K, 6, NX, NY), projected)
```

```python
import functools
import math

import jax
import jax.numpy as jnp
import numpy as np
from jax import lax
from jax.experimental import pallas as pl
from jax.experimental.pallas import tpu as pltpu
from jax.sharding import PartitionSpec as P

MESH = pl.DeviceIdType.MESH
OFFSETS = ((1, 0), (0, 1), (1, 1), (1, -1), (2, 0), (0, 2))
F32 = jnp.float32
BF16 = jnp.bfloat16
COUNT, PARTS, ROWS, LANES = 64, 6, 8, 128
GROUPS = 2
PER = COUNT // GROUPS
BATCH = 4
STEPS_ALL = (-2, -1, 0, 1, 2)
STEPS_HALF = (-1, 0, 1, 2)
NODE_ROWS = PARTS * ROWS


def halo_row(step_y, x):
    return {0: {8: 0, 9: 1, -2: 6, -1: 7}, 1: {8: 3, -1: 2}, -1: {8: 5, -1: 4}}[step_y][x]


def stencil_masks(steps, signs):
    depth = (len(steps) + 1) * NODE_ROWS
    out = np.zeros((len(OFFSETS) * len(signs), ROWS, depth), np.float32)
    for i, sign in enumerate(signs):
        for q, (ox, oy) in enumerate(OFFSETS):
            dx, dy = sign * ox, sign * oy
            for x in range(ROWS):
                for d in range(PARTS):
                    if 0 <= x + dx < ROWS:
                        at = steps.index(dy) * NODE_ROWS + d * ROWS + x + dx
                    else:
                        at = len(steps) * NODE_ROWS + d * ROWS + halo_row(dy, x + dx)
                    out[i * len(OFFSETS) + q, x, at] = 1.0
    return out


def spread(steps):
    depth = (len(steps) + 1) * NODE_ROWS
    out = np.zeros((PARTS, depth), np.float32)
    for at in range(depth):
        out[(at % NODE_ROWS) // ROWS, at] = 1.0
    return out


def split(x):
    hi = x.astype(BF16)
    return hi, (x - hi.astype(F32)).astype(BF16)


def build(coup_ref, spread_value, mask_ref, both, hi_ref, lo_ref):
    rows = [None] * PARTS
    n = len(OFFSETS)
    for s in range(2 * n if both else n):
        block = coup_ref[s % n]
        dims = (((1 if s < n else 0,), (0,)), ((), ()))
        wide = lax.dot_general(
            block, spread_value, dims, precision=lax.Precision.HIGHEST, preferred_element_type=F32
        )
        for c in range(PARTS):
            term = wide[c : c + 1, :] * mask_ref[s]
            rows[c] = term if rows[c] is None else rows[c] + term
    hi, lo = split(jnp.concatenate(rows, axis=0))
    hi_ref[...] = hi
    lo_ref[...] = lo


def stencil_kernel(
    gx, gy,
    dir_ref, scale_ref, mask_ref, srow_ref, scol_ref, center_ref, coup_ref, stiff_ref,
    mask1_ref, spread1_ref, mask2_ref, spread2_ref,
    flat_out, sums_out,
    u, hx, prod, u2, hx2, image,
    pk, pyp, pym, hcp, hcm, pk2, py2p, py2m, hc2p, hc2m,
    m1hi, m1lo, m2hi, m2lo, flat, iflat, zbuf, r1, r2, zall,
    xs_send, xs_recv, ys_send, ys_recv, cs_send, cs_recv,
    a_send, a_recv, b_send, b_recv, c_send, c_recv, out_sem,
):
    ix, iy = lax.axis_index("gx"), lax.axis_index("gy")
    xp, xm = lax.rem(ix + 1, gx), lax.rem(ix + gx - 1, gx)
    yp, ym = lax.rem(iy + 1, gy), lax.rem(iy + gy - 1, gy)

    barrier = pltpu.get_barrier_semaphore()

    def greet(px, py):
        pl.semaphore_signal(barrier, inc=1, device_id=(px, py), device_id_type=MESH)

    for j in range(1, gx):
        greet(lax.rem(ix + j, gx), iy)
    for j in range(1, gy):
        greet(ix, lax.rem(iy + j, gy))
    for px in (xp, xm):
        for py in (yp, ym):
            greet(px, py)

    lane = lax.broadcasted_iota(jnp.int32, (ROWS, LANES), 1)
    row = lax.broadcasted_iota(jnp.int32, (ROWS, LANES), 0)
    mask = mask_ref[...].astype(F32)
    weight = scale_ref[...] * (1.0 - mask)

    def scale_body(i, _):
        g = lax.div(i, PER // BATCH)
        m = lax.rem(i, PER // BATCH) * BATCH
        for c in range(PARTS):
            packed = pk[g * PARTS + c]
            for b in range(BATCH):
                at = (i * BATCH + b) * PARTS + c
                value = weight * dir_ref[at]
                u[at] = value
                moved = pltpu.roll(value, lax.rem(4 * (m + b) + 2, LANES), 1)
                packed = jnp.where(lax.div(lane, 4) == m + b, moved, packed)
            pk[g * PARTS + c] = packed
        return 0

    pk[...] = jnp.zeros_like(pk)
    lax.fori_loop(0, COUNT // BATCH, scale_body, 0)

    def remote(src, dst, send, recv, px, py):
        return pltpu.make_async_remote_copy(
            src_ref=src, dst_ref=dst, send_sem=send, recv_sem=recv,
            device_id=(px, py), device_id_type=MESH,
        )

    pl.semaphore_wait(barrier, (gx - 1) + (gy - 1) + 4)

    def x_copies(src, dst, g, base, down):
        part = pl.ds(g * PER * PARTS, PER * PARTS)
        top = pl.ds(0, 2)
        out = [remote(src.at[part, top], dst.at[part, top], xs_send.at[base], xs_recv.at[base], xm, iy)]
        if down:
            low = pl.ds(6, 2)
            out.append(
                remote(src.at[part, low], dst.at[part, low], xs_send.at[base + 1], xs_recv.at[base + 1], xp, iy)
            )
        return out

    def y_copies(src, dst_p, dst_m, cp, cm, part, base, down):
        first = pl.ds(0, 1)
        last = pl.ds(7, 1)
        out = [
            remote(src.at[part], dst_p.at[part], ys_send.at[base], ys_recv.at[base], ix, ym),
            remote(src.at[part], dst_m.at[part], ys_send.at[base + 1], ys_recv.at[base + 1], ix, yp),
        ]
        k = 2 * base
        out.append(remote(src.at[part, first], cp.at[part, first], cs_send.at[k], cs_recv.at[k], xm, ym))
        out.append(remote(src.at[part, first], cm.at[part, first], cs_send.at[k + 1], cs_recv.at[k + 1], xm, yp))
        if down:
            out.append(remote(src.at[part, last], cp.at[part, last], cs_send.at[k + 2], cs_recv.at[k + 2], xp, ym))
            out.append(remote(src.at[part, last], cm.at[part, last], cs_send.at[k + 3], cs_recv.at[k + 3], xp, yp))
        return out

    y1 = y_copies(pk, pyp, pym, hcp, hcm, pl.ds(0, GROUPS * PARTS), 0, True)
    x1 = [x_copies(u, hx, g, 2 * g, True) for g in range(GROUPS)]
    for copy in y1 + [c for g in x1 for c in g]:
        copy.start()

    rows_hit = jnp.zeros((ROWS, LANES), F32)
    for f in range(srow_ref.shape[0]):
        rows_hit = rows_hit + (row + ix * ROWS == srow_ref[f]).astype(F32)
    cols_hit = jnp.zeros((ROWS, LANES), F32)
    for f in range(scol_ref.shape[0]):
        cols_hit = cols_hit + (lane + iy * LANES == scol_ref[f]).astype(F32)
    build(coup_ref, spread1_ref[...], mask1_ref, True, m1hi, m1lo)
    build(coup_ref, spread2_ref[...], mask2_ref, False, m2hi, m2lo)

    zero = jnp.zeros((ROWS, LANES), F32)
    from_minus = lax.rem(lane, 4) < 2
    in_xp = jnp.full((ROWS, LANES), ix, jnp.int32) < gx - 1
    in_xm = jnp.full((ROWS, LANES), ix, jnp.int32) > 0
    in_yp = jnp.full((ROWS, LANES), iy, jnp.int32) < gy - 1
    in_ym = jnp.full((ROWS, LANES), iy, jnp.int32) > 0
    in_x = (in_xp & (row < 4)) | (in_xm & (row >= 4))
    in_y = (in_ym & from_minus) | (in_yp & (lax.rem(lane, 4) >= 2))

    def merge_y(minus, plus, cminus, cplus, n, start):
        for i in range(n):
            at = start + i
            plus[at] = jnp.where(in_y, jnp.where(from_minus, minus[at], plus[at]), zero)
            cplus[at] = jnp.where(in_y & in_x, jnp.where(from_minus, cminus[at], cplus[at]), zero)

    def windows(source, hx_ref, py_ref, hc_ref, k, g, m, steps, both):
        back = LANES - 2 - 4 * m
        tiles = {s: [] for s in steps}
        halo, centre, down, up = [], [], [], []
        for d in range(PARTS):
            at = k * PARTS + d
            v = source[at]
            h = jnp.where(in_x, hx_ref[at], zero)
            hy = pltpu.roll(py_ref[g * PARTS + d], back, 1)
            hc = pltpu.roll(hc_ref[g * PARTS + d], back, 1)
            for s in steps:
                if s == 0:
                    tiles[s].append(v)
                elif s > 0:
                    tiles[s].append(pltpu.roll(jnp.where(lane < s, hy, v), LANES - s, 1))
                else:
                    tiles[s].append(pltpu.roll(jnp.where(lane >= LANES + s, hy, v), -s, 1))
            right = pltpu.roll(jnp.where(lane < 1, hc, h), LANES - 1, 1)
            left = pltpu.roll(jnp.where(lane >= LANES - 1, hc, h), 1, 1)
            right = pltpu.roll(right, 3, 0)
            left = pltpu.roll(left, 5, 0)
            tile = jnp.where((row == 2) | (row == 3), right, jnp.where((row == 4) | (row == 5), left, h))
            if not both:
                tile = jnp.where((row < 2) | (row == 3) | (row == 5), tile, zero)
            halo.append(tile)
            down.append(pltpu.roll(jnp.where(row < 1, h, v), ROWS - 1, 0))
            if both:
                up.append(pltpu.roll(jnp.where(row >= ROWS - 1, h, v), 1, 0))
        stack = jnp.concatenate([t for s in steps for t in tiles[s]] + halo, axis=0)
        return stack, tiles, down, up

    def couple(stacks, hi_ref, lo_ref):
        hi, lo = split(jnp.concatenate(stacks, axis=1))
        a, b = hi_ref[...], lo_ref[...]
        total = jnp.dot(b, hi, preferred_element_type=F32) + jnp.dot(a, lo, preferred_element_type=F32)
        return total + jnp.dot(a, hi, preferred_element_type=F32)

    def apply_body(g, i, _):
        m = i * BATCH
        first = g * PER + m
        got = [windows(u, hx, pyp, hcp, first + b, g, m + b, STEPS_ALL, True) for b in range(BATCH)]
        total = couple([w[0] for w in got], m1hi, m1lo)
        for c in range(PARTS):
            packed = pk2[g * PARTS + c]
            frame = stiff_ref[0, c] * rows_hit
            stringer = stiff_ref[1, c] * cols_hit
            local = center_ref[c] + 2.0 * frame + 2.0 * stringer
            for b in range(BATCH):
                _, tiles, down, up = got[b]
                v = total[c * ROWS : (c + 1) * ROWS, b * LANES : (b + 1) * LANES]
                v = v + local * tiles[0][c]
                v = v - frame * (tiles[1][c] + tiles[-1][c]) - stringer * (down[c] + up[c])
                at = (first + b) * PARTS + c
                value = weight * v + mask * dir_ref[at]
                prod[pl.ds(pl.multiple_of(at * ROWS, ROWS), ROWS), :] = value
                scaled = weight * value
                u2[at] = scaled
                moved = pltpu.roll(scaled, lax.rem(4 * (m + b) + 2, LANES), 1)
                packed = jnp.where(lax.div(lane, 4) == m + b, moved, packed)
            pk2[g * PARTS + c] = packed
        return 0

    pk2[...] = jnp.zeros_like(pk2)
    for copy in y1:
        copy.wait_recv()
    merge_y(pym, pyp, hcm, hcp, GROUPS * PARTS, 0)
    second = []
    for g in range(GROUPS):
        for copy in x1[g]:
            copy.wait_recv()
        lax.fori_loop(0, PER // BATCH, functools.partial(apply_body, g), 0)
        x2 = x_copies(u2, hx2, g, 2 * GROUPS + g, False)
        y2 = y_copies(pk2, py2p, py2m, hc2p, hc2m, pl.ds(g * PARTS, PARTS), 2 + 2 * g, False)
        for copy in y2 + x2:
            copy.start()
        second.append(y2 + x2)

    for at in range(NODE_ROWS):
        hi, lo = split(prod[pl.ds(at, COUNT, stride=NODE_ROWS), :])
        flat[0:COUNT, at * LANES : (at + 1) * LANES] = hi
        flat[COUNT : 2 * COUNT, at * LANES : (at + 1) * LANES] = lo
    keep = pltpu.make_async_copy(flat, flat_out, out_sem)
    keep.start()
    across = (((1,), (1,)), ((), ()))
    big = lax.dot_general(flat[...], flat[...], across, preferred_element_type=F32)
    fold = big[0:COUNT] + big[COUNT : 2 * COUNT]
    gram = fold[:, 0:COUNT] + fold[:, COUNT : 2 * COUNT]

    def image_body(g, i, _):
        m = i * BATCH
        first = g * PER + m
        got = [windows(u2, hx2, py2p, hc2p, first + b, g, m + b, STEPS_HALF, False) for b in range(BATCH)]
        total = couple([w[0] for w in got], m2hi, m2lo)
        for c in range(PARTS):
            frame = stiff_ref[0, c] * rows_hit
            stringer = stiff_ref[1, c] * cols_hit
            local = 0.5 * center_ref[c] + frame + stringer
            for b in range(BATCH):
                _, tiles, down, _ = got[b]
                v = total[c * ROWS : (c + 1) * ROWS, b * LANES : (b + 1) * LANES]
                v = v + local * tiles[0][c] - frame * tiles[1][c] - stringer * down[c]
                at = pl.ds(pl.multiple_of(((first + b) * PARTS + c) * ROWS, ROWS), ROWS)
                image[at, :] = weight * v + (0.5 * mask) * prod[at, :]
        return 0

    for g in range(GROUPS):
        for copy in second[g]:
            copy.wait_recv()
        merge_y(py2m, py2p, hc2m, hc2p, PARTS, g * PARTS)
        lax.fori_loop(0, PER // BATCH, functools.partial(image_body, g), 0)
    for at in range(NODE_ROWS):
        hi, lo = split(image[pl.ds(at, COUNT, stride=NODE_ROWS), :])
        iflat[0:COUNT, at * LANES : (at + 1) * LANES] = hi
        iflat[COUNT : 2 * COUNT, at * LANES : (at + 1) * LANES] = lo
    big = lax.dot_general(flat[...], iflat[...], across, preferred_element_type=F32)
    fold = big[0:COUNT] + big[COUNT : 2 * COUNT]
    half = fold[:, 0:COUNT] + fold[:, COUNT : 2 * COUNT]

    both = jnp.concatenate([gram, half], axis=1)
    size = COUNT // gx
    for j in range(gx):
        zbuf[j] = both[j * size : (j + 1) * size, :]
    sends = []
    for j in range(1, gx):
        to = lax.rem(ix + j, gx)
        sends.append(remote(zbuf.at[to], r1.at[j], a_send.at[j], a_recv.at[j], to, iy))
    for copy in sends:
        copy.start()
    part = zbuf[ix]
    for j in range(1, gx):
        sends[j - 1].wait_recv()
        part = part + r1[j]
    r2[iy] = part
    swaps = []
    for j in range(1, gy):
        to = lax.rem(iy + j, gy)
        swaps.append(remote(r2.at[iy], r2.at[iy], b_send.at[j], b_recv.at[j], ix, to))
    for copy in swaps:
        copy.start()
    for copy in swaps:
        copy.wait_recv()
    part = r2[0]
    for j in range(1, gy):
        part = part + r2[j]
    zall[ix] = part
    gathers = []
    for j in range(1, gx):
        to = lax.rem(ix + j, gx)
        gathers.append(remote(zall.at[ix], zall.at[ix], c_send.at[j], c_recv.at[j], to, iy))
    for copy in gathers:
        copy.start()
    for copy in gathers:
        copy.wait_recv()
    for j in range(gx):
        sums_out[j * size : (j + 1) * size, :] = zall[j]
    for copy in y1 + [c for g in x1 for c in g] + [c for g in second for c in g] + sends + swaps + gathers:
        copy.wait_send()
    keep.wait()


def finish_kernel(scale, sums_ref, flat_hbm, basis_ref, projected_ref, flat, sem):
    fetch = pltpu.make_async_copy(flat_hbm, flat, sem)
    fetch.start()
    sums = sums_ref[...]
    half = sums[:, COUNT : 2 * COUNT]
    cross = half + half.T
    lane = lax.broadcasted_iota(jnp.int32, (ROWS, LANES), 1)
    row = lax.broadcasted_iota(jnp.int32, (ROWS, LANES), 0)
    tiles = []
    for i in range(COUNT // ROWS):
        unit = (lane == COUNT + row + i * ROWS).astype(F32)
        tiles.append(jnp.where(lane < COUNT, sums[i * ROWS : (i + 1) * ROWS, :], unit))
    done = []
    for p in range(COUNT):
        block, inside = p // ROWS, p % ROWS
        pivot_row = tiles[block][inside : inside + 1, :]
        pivot = pivot_row[:, p : p + 1]
        done.append(pivot_row * lax.rsqrt(pivot))
        scaled_row = pivot_row / pivot
        for i in range(block, COUNT // ROWS):
            col = tiles[i][:, p : p + 1]
            if i == block:
                col = jnp.where(row > inside, col, 0.0)
            tiles[i] = tiles[i] - col * scaled_row
    whole = jnp.concatenate(done, axis=0)
    inverse_t = whole[:, COUNT : 2 * COUNT]
    left = jnp.dot(inverse_t, cross, precision=lax.Precision.HIGHEST, preferred_element_type=F32)
    projected_ref[...] = lax.dot_general(
        left, inverse_t, (((1,), (1,)), ((), ())), precision=lax.Precision.HIGHEST, preferred_element_type=F32
    )
    hi, lo = split(scale * inverse_t)
    fetch.wait()
    twice = jnp.concatenate([hi, hi], axis=1)
    for at in range(NODE_ROWS):
        cols = slice(at * LANES, (at + 1) * LANES)
        value = jnp.dot(twice, flat[:, cols], preferred_element_type=F32)
        value = value + jnp.dot(lo, flat[0:COUNT, cols], preferred_element_type=F32)
        basis_ref[pl.ds(at, COUNT, stride=NODE_ROWS), :] = value


def body(gx, gy, directions, node_scale, boundary_mask, stiffener_rows, stiffener_cols, center, couplings, stiffness):
    tiles = COUNT * PARTS
    nodes = NODE_ROWS * LANES
    size = COUNT // gx
    vmem = pl.BlockSpec(memory_space=pltpu.VMEM)
    smem = pl.BlockSpec(memory_space=pltpu.SMEM)
    hbm = pl.BlockSpec(memory_space=pl.ANY)
    depth1 = (len(STEPS_ALL) + 1) * NODE_ROWS
    depth2 = (len(STEPS_HALF) + 1) * NODE_ROWS
    field = pltpu.VMEM((tiles, ROWS, LANES), F32)
    plain = pltpu.VMEM((tiles * ROWS, LANES), F32)
    edge = pltpu.VMEM((GROUPS * PARTS, ROWS, LANES), F32)
    dma = pltpu.SemaphoreType.DMA
    flat, sums = pl.pallas_call(
        functools.partial(stencil_kernel, gx, gy),
        out_shape=(
            jax.ShapeDtypeStruct((2 * COUNT, nodes), BF16),
            jax.ShapeDtypeStruct((COUNT, 2 * COUNT), F32),
        ),
        in_specs=[vmem, vmem, vmem, smem, smem, smem, vmem, smem, vmem, vmem, vmem, vmem],
        out_specs=(hbm, vmem),
        scratch_shapes=[
            field, field, plain, field, field, plain,
            edge, edge, edge, edge, edge, edge, edge, edge, edge, edge,
            pltpu.VMEM((NODE_ROWS, depth1), BF16), pltpu.VMEM((NODE_ROWS, depth1), BF16),
            pltpu.VMEM((NODE_ROWS, depth2), BF16), pltpu.VMEM((NODE_ROWS, depth2), BF16),
            pltpu.VMEM((2 * COUNT, nodes), BF16), pltpu.VMEM((2 * COUNT, nodes), BF16),
            pltpu.VMEM((gx, size, LANES), F32), pltpu.VMEM((gx, size, LANES), F32),
            pltpu.VMEM((gy, size, LANES), F32), pltpu.VMEM((gx, size, LANES), F32),
            dma((3 * GROUPS,)), dma((3 * GROUPS,)),
            dma((2 + 2 * GROUPS,)), dma((2 + 2 * GROUPS,)),
            dma((4 + 4 * GROUPS,)), dma((4 + 4 * GROUPS,)),
            dma((gx,)), dma((gx,)), dma((gy,)), dma((gy,)), dma((gx,)), dma((gx,)),
            dma(()),
        ],
        compiler_params=pltpu.CompilerParams(
            collective_id=0, has_side_effects=True, vmem_limit_bytes=48 * 1024 * 1024
        ),
        name="stencil",
    )(
        directions.reshape(tiles, ROWS, LANES), node_scale, boundary_mask, stiffener_rows, stiffener_cols,
        center, couplings, stiffness,
        jnp.asarray(stencil_masks(STEPS_ALL, (1, -1))), jnp.asarray(spread(STEPS_ALL)),
        jnp.asarray(stencil_masks(STEPS_HALF, (1,))), jnp.asarray(spread(STEPS_HALF)),
    )
    scale = math.sqrt(PARTS * gx * ROWS * gy * LANES)
    basis, projected = pl.pallas_call(
        functools.partial(finish_kernel, scale),
        out_shape=(
            jax.ShapeDtypeStruct((tiles * ROWS, LANES), F32),
            jax.ShapeDtypeStruct((COUNT, COUNT), F32),
        ),
        in_specs=[vmem, hbm],
        out_specs=(vmem, vmem),
        scratch_shapes=[pltpu.VMEM((2 * COUNT, nodes), BF16), dma(())],
        compiler_params=pltpu.CompilerParams(vmem_limit_bytes=48 * 1024 * 1024),
        name="finish",
    )(sums, flat)
    return basis.reshape(COUNT, PARTS, ROWS, LANES), projected


def solution(mesh):
    gx, gy = mesh.shape["gx"], mesh.shape["gy"]
    in_specs = (P(None, None, "gx", "gy"), P("gx", "gy"), P("gx", "gy"), P(), P(), P(), P(), P())
    out_specs = (P(None, None, "gx", "gy"), P())
    return jax.shard_map(
        functools.partial(body, gx, gy), mesh=mesh, in_specs=in_specs, out_specs=out_specs, check_vma=False
    )
```

```python
import functools
import math

import jax
import jax.numpy as jnp
import numpy as np
from jax import lax
from jax.experimental import pallas as pl
from jax.experimental.pallas import tpu as pltpu
from jax.sharding import PartitionSpec as P

MESH = pl.DeviceIdType.MESH
OFFSETS = ((1, 0), (0, 1), (1, 1), (1, -1), (2, 0), (0, 2))
F32 = jnp.float32
BF16 = jnp.bfloat16
COUNT, PARTS, ROWS, LANES = 64, 6, 8, 128
CROSS_STEP = 48
PIECES = 8
GROUPS = 2
PER = COUNT // GROUPS
BATCH = 8
STEPS = (-1, 0, 1, 2)
NODE_ROWS = PARTS * ROWS


def halo_row(step_y, x):
    return {0: {8: 0, 9: 1, -2: 6, -1: 7}, 1: {8: 3, -1: 2}, -1: {8: 5, -1: 4}}[step_y][x]


DEPTH = (len(STEPS) + 1) * NODE_ROWS


def stencil_masks():
    n = len(OFFSETS)
    out = np.zeros((2 * n, ROWS, DEPTH), np.float32)
    for i, sign in enumerate((1, -1)):
        for q, (ox, oy) in enumerate(OFFSETS):
            dx, dy = sign * ox, sign * oy
            for x in range(ROWS):
                for d in range(PARTS):
                    if dy not in STEPS:
                        continue
                    if 0 <= x + dx < ROWS:
                        at = STEPS.index(dy) * NODE_ROWS + d * ROWS + x + dx
                    else:
                        at = len(STEPS) * NODE_ROWS + d * ROWS + halo_row(dy, x + dx)
                    out[i * n + q, x, at] = 1.0
    return out


def spread():
    out = np.zeros((PARTS, DEPTH), np.float32)
    for at in range(DEPTH):
        out[(at % NODE_ROWS) // ROWS, at] = 1.0
    return out


def split(x):
    hi = x.astype(BF16)
    return hi, (x - hi.astype(F32)).astype(BF16)


def build(coup_ref, spread_ref, mask_ref, both, out_ref):
    n = len(OFFSETS)
    expand = spread_ref[...]
    rows, beside = [None] * PARTS, []
    for s in range(2 * n - 1 if both else n):
        dims = (((1 if s < n else 0,), (0,)), ((), ()))
        wide = lax.dot_general(
            coup_ref[s % n], expand, dims, precision=lax.Precision.HIGHEST, preferred_element_type=F32
        )
        for c in range(PARTS):
            term = wide[c : c + 1, :] * mask_ref[s]
            rows[c] = term if rows[c] is None else rows[c] + term
    near = mask_ref[0] + mask_ref[n] if both else mask_ref[0]
    for c in range(PARTS):
        beside.append(expand[c : c + 1, :] * near)
    hi, lo = split(jnp.concatenate(rows, axis=0))
    out_ref[0:NODE_ROWS] = hi
    out_ref[NODE_ROWS : 2 * NODE_ROWS] = jnp.concatenate(beside, axis=0).astype(BF16)
    out_ref[2 * NODE_ROWS :] = lo


def stencil_kernel(
    gx, gy,
    dir_hbm, scale_hbm, mask_hbm, srow_hbm, scol_hbm, center_hbm, coup_hbm, stiff_hbm,
    masks_hbm, spread_hbm,
    basis_out, projected_ref,
    dir_ref, scale_ref, mask_ref, srow_ref, scol_ref, center_ref, coup_ref, stiff_ref,
    masks_ref, spread_ref, in_sems, dir_sems,
    u, hx, prod, u2, hx2, image,
    pk, pyp, pym, hcp, hcm, pk2, py2p, py2m, hc2p, hc2m,
    m1, m2, far_coup, flat, iflat, g_own, g_a, g_b, c_own, c_a, c_b, basis,
    xs_send, xs_recv, ys_send, ys_recv, cs_send, cs_recv,
    ga_send, ga_recv, gb_send, gb_recv, ca_send, ca_recv, cb_send, cb_recv, out_sem,
):
    small = [
        pltpu.make_async_copy(src, dst, in_sems.at[i])
        for i, (src, dst) in enumerate((
            (scale_hbm, scale_ref), (mask_hbm, mask_ref), (srow_hbm, srow_ref), (scol_hbm, scol_ref),
            (center_hbm, center_ref), (coup_hbm, coup_ref), (stiff_hbm, stiff_ref), (masks_hbm, masks_ref),
            (spread_hbm, spread_ref),
        ))
    ]
    large = []
    for i in range(GROUPS):
        part = pl.ds(i * PER * PARTS, PER * PARTS)
        large.append(pltpu.make_async_copy(dir_hbm.at[part], dir_ref.at[part], dir_sems.at[i]))
    for copy in small[:2] + large + small[2:]:
        copy.start()
    ix, iy = lax.axis_index("gx"), lax.axis_index("gy")
    xp, xm = lax.rem(ix + 1, gx), lax.rem(ix + gx - 1, gx)
    yp, ym = lax.rem(iy + 1, gy), lax.rem(iy + gy - 1, gy)

    barrier = pltpu.get_barrier_semaphore()

    def greet(px, py):
        pl.semaphore_signal(barrier, inc=1, device_id=(px, py), device_id_type=MESH)

    na, nb = gx // 2, 2 * gy
    ia, ib = lax.rem(ix, na), lax.div(ix, na) * gy + iy

    def peer_a(j):
        return lax.div(ix, na) * na + lax.rem(ia + j, na), iy

    def peer_b(j):
        to = lax.rem(ib + j, nb)
        return lax.div(to, gy) * na + ia, lax.rem(to, gy)

    for j in range(1, na):
        greet(*peer_a(j))
    for j in range(1, nb):
        greet(*peer_b(j))
    for px in (xp, xm):
        greet(px, iy)
        for py in (yp, ym):
            greet(px, py)
    for py in (yp, ym):
        greet(ix, py)

    lane = lax.broadcasted_iota(jnp.int32, (ROWS, LANES), 1)
    row = lax.broadcasted_iota(jnp.int32, (ROWS, LANES), 0)
    small[0].wait()
    small[1].wait()
    mask = mask_ref[...].astype(F32)
    weight = scale_ref[...] * (1.0 - mask)

    def scale_body(i, _):
        g = lax.div(i, PER // BATCH)
        m = lax.rem(i, PER // BATCH) * BATCH
        for c in range(PARTS):
            packed = pk[g * PARTS + c]
            for b in range(BATCH):
                at = (i * BATCH + b) * PARTS + c
                value = weight * dir_ref[at]
                u[at] = value
                moved = pltpu.roll(value, lax.rem(4 * (m + b) + 2, LANES), 1)
                packed = jnp.where(lax.div(lane, 4) == m + b, moved, packed)
            pk[g * PARTS + c] = packed
        return 0

    pk[...] = jnp.zeros_like(pk)
    for g in range(GROUPS):
        large[g].wait()
        lax.fori_loop(g * PER // BATCH, (g + 1) * PER // BATCH, scale_body, 0)

    def remote(src, dst, send, recv, px, py):
        return pltpu.make_async_remote_copy(
            src_ref=src, dst_ref=dst, send_sem=send, recv_sem=recv,
            device_id=(px, py), device_id_type=MESH,
        )

    pl.semaphore_wait(barrier, (na - 1) + (nb - 1) + 8)

    def x_copies(src, dst, g, base, down):
        part = pl.ds(g * PER * PARTS, PER * PARTS)
        top = pl.ds(0, 2)
        out = [remote(src.at[part, top], dst.at[part, top], xs_send.at[base], xs_recv.at[base], xm, iy)]
        if down:
            low = pl.ds(6, 2)
            out.append(
                remote(src.at[part, low], dst.at[part, low], xs_send.at[base + 1], xs_recv.at[base + 1], xp, iy)
            )
        return out

    def y_copies(src, dst_p, dst_m, cp, cm, part, base, down):
        first = pl.ds(0, 1)
        last = pl.ds(7, 1)
        out = [
            remote(src.at[part], dst_p.at[part], ys_send.at[base], ys_recv.at[base], ix, ym),
            remote(src.at[part], dst_m.at[part], ys_send.at[base + 1], ys_recv.at[base + 1], ix, yp),
        ]
        k = 2 * base
        out.append(remote(src.at[part, first], cp.at[part, first], cs_send.at[k], cs_recv.at[k], xm, ym))
        out.append(remote(src.at[part, first], cm.at[part, first], cs_send.at[k + 1], cs_recv.at[k + 1], xm, yp))
        if down:
            out.append(remote(src.at[part, last], cp.at[part, last], cs_send.at[k + 2], cs_recv.at[k + 2], xp, ym))
            out.append(remote(src.at[part, last], cm.at[part, last], cs_send.at[k + 3], cs_recv.at[k + 3], xp, yp))
        return out

    y1 = y_copies(pk, pyp, pym, hcp, hcm, pl.ds(0, GROUPS * PARTS), 0, True)
    x1 = [x_copies(u, hx, g, 2 * g, True) for g in range(GROUPS)]
    for copy in y1 + [c for g in x1 for c in g]:
        copy.start()

    for copy in small[2:]:
        copy.wait()

    rows_hit = jnp.zeros((ROWS, LANES), F32)
    for f in range(srow_ref.shape[0]):
        rows_hit = rows_hit + (row + ix * ROWS == srow_ref[f]).astype(F32)
    cols_hit = jnp.zeros((ROWS, LANES), F32)
    for f in range(scol_ref.shape[0]):
        cols_hit = cols_hit + (lane + iy * LANES == scol_ref[f]).astype(F32)
    build(coup_ref, spread_ref, masks_ref, True, m1)
    build(coup_ref, spread_ref, masks_ref, False, m2)
    last = coup_ref[len(OFFSETS) - 1]
    for c in range(PARTS):
        for d in range(PARTS):
            far_coup[c * PARTS + d] = jnp.broadcast_to(last[d : d + 1, c : c + 1], (ROWS, LANES))

    zero = jnp.zeros((ROWS, LANES), F32)
    from_minus = lax.rem(lane, 4) < 2
    in_xp = jnp.full((ROWS, LANES), ix, jnp.int32) < gx - 1
    in_xm = jnp.full((ROWS, LANES), ix, jnp.int32) > 0
    in_yp = jnp.full((ROWS, LANES), iy, jnp.int32) < gy - 1
    in_ym = jnp.full((ROWS, LANES), iy, jnp.int32) > 0
    in_x = (in_xp & (row < 4)) | (in_xm & (row >= 4))
    in_x2 = in_xp & (row < 2)
    in_y = (in_ym & from_minus) | (in_yp & (lax.rem(lane, 4) >= 2))

    def merge_y(minus, plus, cminus, cplus, n, start, in_corner):
        for i in range(n):
            at = start + i
            plus[at] = jnp.where(in_y, jnp.where(from_minus, minus[at], plus[at]), zero)
            cplus[at] = jnp.where(in_y & in_corner, jnp.where(from_minus, cminus[at], cplus[at]), zero)

    def windows(source, hx_ref, py_ref, hc_ref, k, g, m, inside, both):
        back = LANES - 2 - 4 * m
        tiles = {s: [] for s in STEPS}
        halo, far = [], []
        for d in range(PARTS):
            at = k * PARTS + d
            v = source[at]
            h = jnp.where(inside, hx_ref[at], zero)
            hy = pltpu.roll(py_ref[g * PARTS + d], back, 1)
            hc = pltpu.roll(hc_ref[g * PARTS + d], back, 1)
            for s in STEPS:
                if s == 0:
                    tiles[s].append(v)
                elif s > 0:
                    tiles[s].append(pltpu.roll(jnp.where(lane < s, hy, v), LANES - s, 1))
                else:
                    tiles[s].append(pltpu.roll(jnp.where(lane >= LANES + s, hy, v), -s, 1))
            if both:
                far.append(pltpu.roll(jnp.where(lane >= LANES - 2, hy, v), 2, 1))
            right = pltpu.roll(jnp.where(lane < 1, hc, h), LANES - 1, 1)
            left = pltpu.roll(jnp.where(lane >= LANES - 1, hc, h), 1, 1)
            right = pltpu.roll(right, 3, 0)
            left = pltpu.roll(left, 5, 0)
            halo.append(jnp.where((row == 2) | (row == 3), right, jnp.where((row == 4) | (row == 5), left, h)))
        stack = jnp.concatenate([t for s in STEPS for t in tiles[s]] + halo, axis=0)
        return stack, tiles, far

    def couple(stacks, m_ref):
        hi, lo = split(jnp.concatenate(stacks, axis=1))
        top = jnp.dot(m_ref[...], hi, preferred_element_type=F32)
        low = jnp.dot(m_ref[0 : 2 * NODE_ROWS], lo, preferred_element_type=F32)
        return top[0:NODE_ROWS] + (top[2 * NODE_ROWS :] + low[0:NODE_ROWS]), (
            top[NODE_ROWS : 2 * NODE_ROWS] + low[NODE_ROWS:]
        )

    def tile_of(x, c, b):
        return x[c * ROWS : (c + 1) * ROWS, b * LANES : (b + 1) * LANES]

    def apply_body(g, i, _):
        m = i * BATCH
        first = g * PER + m
        got = [windows(u, hx, pyp, hcp, first + b, g, m + b, in_x, True) for b in range(BATCH)]
        total, beside = couple([w[0] for w in got], m1)
        for c in range(PARTS):
            packed = pk2[g * PARTS + c]
            frame = stiff_ref[0, c] * rows_hit
            stringer = stiff_ref[1, c] * cols_hit
            local = center_ref[c] + 2.0 * frame + 2.0 * stringer
            for b in range(BATCH):
                _, tiles, far = got[b]
                v = tile_of(total, c, b) + local * tiles[0][c]
                v = v - frame * (tiles[1][c] + tiles[-1][c]) - stringer * tile_of(beside, c, b)
                for d in range(PARTS):
                    v = v + far_coup[c * PARTS + d] * far[d]
                at = (first + b) * PARTS + c
                value = weight * v + mask * dir_ref[at]
                prod[pl.ds(pl.multiple_of(at * ROWS, ROWS), ROWS), :] = value
                scaled = weight * value
                u2[at] = scaled
                moved = pltpu.roll(scaled, lax.rem(4 * (m + b) + 2, LANES), 1)
                packed = jnp.where(lax.div(lane, 4) == m + b, moved, packed)
            pk2[g * PARTS + c] = packed
        return 0

    pk2[...] = jnp.zeros_like(pk2)
    for copy in y1:
        copy.wait_recv()
    merge_y(pym, pyp, hcm, hcp, GROUPS * PARTS, 0, in_x)
    second = []
    for g in range(GROUPS):
        for copy in x1[g]:
            copy.wait_recv()
        lax.fori_loop(0, PER // BATCH, functools.partial(apply_body, g), 0)
        x2 = x_copies(u2, hx2, g, 2 * GROUPS + g, False)
        y2 = y_copies(pk2, py2p, py2m, hc2p, hc2m, pl.ds(g * PARTS, PARTS), 2 + 2 * g, False)
        for copy in y2 + x2:
            copy.start()
        second.append(y2 + x2)

    def send_all(own, slots, mine, peer, count, send, recv):
        copies = []
        for j in range(1, count):
            copies.append(remote(own, slots.at[mine], send.at[j], recv.at[j], *peer(j)))
        for copy in copies:
            copy.start()
        return copies

    def receive_sum(copies, own, slots, mine, count):
        slots[mine] = own[...]
        for copy in copies:
            copy.wait_recv()
        total = slots[0]
        for j in range(1, count):
            total = total + slots[j]
        return total

    def regroup(source, target):
        for at in range(NODE_ROWS):
            hi, lo = split(source[pl.ds(at, COUNT, stride=NODE_ROWS), :])
            target[0:COUNT, at * LANES : (at + 1) * LANES] = hi
            target[COUNT : 2 * COUNT, at * LANES : (at + 1) * LANES] = lo

    def inner(left, right):
        big = lax.dot_general(left[...], right[...], (((1,), (1,)), ((), ())), preferred_element_type=F32)
        fold = big[0:COUNT] + big[COUNT : 2 * COUNT]
        fold = fold[:, 0:COUNT] + fold[:, COUNT : 2 * COUNT]
        return jnp.concatenate([fold[0 : COUNT // 2], fold[COUNT // 2 :]], axis=1)

    def unfold(x):
        return jnp.concatenate([x[:, 0:COUNT], x[:, COUNT : 2 * COUNT]], axis=0)

    regroup(prod, flat)
    g_own[0] = inner(flat, flat)
    g_first = send_all(g_own.at[0], g_a, ia, peer_a, na, ga_send, ga_recv)

    def image_body(g, i, _):
        m = i * BATCH
        first = g * PER + m
        got = [windows(u2, hx2, py2p, hc2p, first + b, g, m + b, in_x2, False) for b in range(BATCH)]
        total, beside = couple([w[0] for w in got], m2)
        for c in range(PARTS):
            frame = stiff_ref[0, c] * rows_hit
            stringer = stiff_ref[1, c] * cols_hit
            local = 0.5 * center_ref[c] + frame + stringer
            for b in range(BATCH):
                _, tiles, _ = got[b]
                v = tile_of(total, c, b) + local * tiles[0][c]
                v = v - frame * tiles[1][c] - stringer * tile_of(beside, c, b)
                at = pl.ds(pl.multiple_of(((first + b) * PARTS + c) * ROWS, ROWS), ROWS)
                image[at, :] = weight * v + (0.5 * mask) * prod[at, :]
        return 0

    for g in range(GROUPS):
        for copy in second[g]:
            copy.wait_recv()
        merge_y(py2m, py2p, hc2m, hc2p, PARTS, g * PARTS, in_x2)
        lax.fori_loop(0, PER // BATCH, functools.partial(image_body, g), 0)
        if g == 0:
            g_own[1] = receive_sum(g_first, g_own.at[0], g_a, ia, na)
            g_second = send_all(g_own.at[1], g_b, ib, peer_b, nb, gb_send, gb_recv)
    regroup(image, iflat)
    c_own[0] = inner(flat, iflat)
    c_first = send_all(c_own.at[0], c_a, ia, peer_a, na, ca_send, ca_recv)

    gram = unfold(receive_sum(g_second, g_own.at[1], g_b, ib, nb))
    tiles = []
    for i in range(COUNT // ROWS):
        unit = (lax.broadcasted_iota(jnp.int32, (ROWS, COUNT), 1) == i * ROWS
                + lax.broadcasted_iota(jnp.int32, (ROWS, COUNT), 0)).astype(F32)
        tiles.append(jnp.concatenate([gram[i * ROWS : (i + 1) * ROWS], unit], axis=1))
    done = []
    for p in range(COUNT):
        if p == CROSS_STEP:
            c_own[1] = receive_sum(c_first, c_own.at[0], c_a, ia, na)
            c_second = send_all(c_own.at[1], c_b, ib, peer_b, nb, cb_send, cb_recv)
        block, inside = p // ROWS, p % ROWS
        pivot_row = tiles[block][inside : inside + 1, :]
        pivot = pivot_row[:, p : p + 1]
        done.append(pivot_row * lax.rsqrt(pivot))
        scaled_row = pivot_row / pivot
        for i in range(block, COUNT // ROWS):
            col = tiles[i][:, p : p + 1]
            if i == block:
                col = jnp.where(row > inside, col, 0.0)
            tiles[i] = tiles[i] - col * scaled_row
    inverse_t = jnp.concatenate(done, axis=0)[:, COUNT : 2 * COUNT]

    scale = math.sqrt(PARTS * gx * ROWS * gy * LANES)
    hi, lo = split(scale * inverse_t)
    factors = jnp.concatenate([hi, hi, lo], axis=1)
    width = 2 * LANES
    for i in range(NODE_ROWS // 2):
        cols = slice(i * width, (i + 1) * width)
        fields = jnp.concatenate([flat[:, cols], flat[0:COUNT, cols]], axis=0)
        value = jnp.dot(factors, fields, preferred_element_type=F32)
        for j in range(2):
            basis[pl.ds(2 * i + j, COUNT, stride=NODE_ROWS), :] = value[:, j * LANES : (j + 1) * LANES]
    keep = pltpu.make_async_copy(basis, basis_out, out_sem)
    keep.start()

    half = unfold(receive_sum(c_second, c_own.at[1], c_b, ib, nb))
    cross = half + half.T
    left = jnp.dot(inverse_t, cross, precision=lax.Precision.HIGHEST, preferred_element_type=F32)
    projected_ref[...] = lax.dot_general(
        left, inverse_t, (((1,), (1,)), ((), ())), precision=lax.Precision.HIGHEST, preferred_element_type=F32
    )
    for copy in y1 + [c for g in x1 for c in g] + [c for g in second for c in g]:
        copy.wait_send()
    for copy in g_first + g_second + c_first + c_second:
        copy.wait_send()
    keep.wait()


def hand_over_kernel(basis_in, projected_in, basis_out, projected_out, basis, projected, in_sems, out_sems):
    rows = basis_in.shape[0] // PIECES
    ways = [(basis_in.at[part], basis.at[part], basis_out.at[part])
            for part in (pl.ds(i * rows, rows) for i in range(PIECES))]
    ways.append((projected_in, projected, projected_out))
    arrive = [pltpu.make_async_copy(a, b, in_sems.at[i]) for i, (a, b, _) in enumerate(ways)]
    leave = [pltpu.make_async_copy(b, c, out_sems.at[i]) for i, (_, b, c) in enumerate(ways)]
    for copy in arrive:
        copy.start()
    for first, then in zip(arrive, leave):
        first.wait()
        then.start()
    for copy in leave:
        copy.wait()


def body(gx, gy, directions, node_scale, boundary_mask, stiffener_rows, stiffener_cols, center, couplings, stiffness):
    tiles = COUNT * PARTS
    nodes = NODE_ROWS * LANES
    na, nb = gx // 2, 2 * gy
    vmem = pl.BlockSpec(memory_space=pltpu.VMEM)
    hbm = pl.BlockSpec(memory_space=pl.ANY)
    field = pltpu.VMEM((tiles, ROWS, LANES), F32)
    plain = pltpu.VMEM((tiles * ROWS, LANES), F32)
    edge = pltpu.VMEM((GROUPS * PARTS, ROWS, LANES), F32)
    parts = pltpu.VMEM((2 * COUNT, nodes), BF16)
    matrix = pltpu.VMEM((3 * NODE_ROWS, DEPTH), BF16)
    small = (COUNT // 2, 2 * COUNT)
    dma = pltpu.SemaphoreType.DMA
    basis, projected = pl.pallas_call(
        functools.partial(stencil_kernel, gx, gy),
        out_shape=(
            jax.ShapeDtypeStruct((tiles * ROWS, LANES), F32),
            jax.ShapeDtypeStruct((COUNT, COUNT), F32),
        ),
        in_specs=[hbm] * 10,
        out_specs=(hbm, vmem),
        scratch_shapes=[
            field, pltpu.VMEM((ROWS, LANES), F32), pltpu.VMEM((ROWS, LANES), jnp.int32),
            pltpu.SMEM(stiffener_rows.shape, jnp.int32), pltpu.SMEM(stiffener_cols.shape, jnp.int32),
            pltpu.SMEM((PARTS,), F32), pltpu.VMEM((len(OFFSETS), PARTS, PARTS), F32), pltpu.SMEM((2, PARTS), F32),
            pltpu.VMEM((2 * len(OFFSETS), ROWS, DEPTH), F32), pltpu.VMEM((PARTS, DEPTH), F32),
            dma((9,)), dma((GROUPS,)),
            field, field, plain, field, field, plain,
            edge, edge, edge, edge, edge, edge, edge, edge, edge, edge,
            matrix, matrix, pltpu.VMEM((PARTS * PARTS, ROWS, LANES), F32), parts, parts,
            pltpu.VMEM((2,) + small, F32), pltpu.VMEM((na,) + small, F32), pltpu.VMEM((nb,) + small, F32),
            pltpu.VMEM((2,) + small, F32), pltpu.VMEM((na,) + small, F32), pltpu.VMEM((nb,) + small, F32),
            plain,
            dma((3 * GROUPS,)), dma((3 * GROUPS,)),
            dma((2 + 2 * GROUPS,)), dma((2 + 2 * GROUPS,)),
            dma((4 + 4 * GROUPS,)), dma((4 + 4 * GROUPS,)),
            dma((na,)), dma((na,)), dma((nb,)), dma((nb,)),
            dma((na,)), dma((na,)), dma((nb,)), dma((nb,)),
            dma(()),
        ],
        compiler_params=pltpu.CompilerParams(
            collective_id=0, has_side_effects=True, vmem_limit_bytes=63 * 1024 * 1024
        ),
        name="stencil",
    )(
        directions.reshape(tiles, ROWS, LANES), node_scale, boundary_mask, stiffener_rows, stiffener_cols,
        center, couplings, stiffness, jnp.asarray(stencil_masks()), jnp.asarray(spread()),
    )
    basis, projected = pl.pallas_call(
        hand_over_kernel,
        out_shape=(
            jax.ShapeDtypeStruct((tiles * ROWS, LANES), F32),
            jax.ShapeDtypeStruct((COUNT, COUNT), F32),
        ),
        in_specs=[hbm, hbm],
        out_specs=(hbm, hbm),
        scratch_shapes=[plain, pltpu.VMEM((COUNT, COUNT), F32), dma((PIECES + 1,)), dma((PIECES + 1,))],
        compiler_params=pltpu.CompilerParams(vmem_limit_bytes=63 * 1024 * 1024),
        name="hand_over",
    )(basis, projected)
    return basis.reshape(COUNT, PARTS, ROWS, LANES), projected


def solution(mesh):
    gx, gy = mesh.shape["gx"], mesh.shape["gy"]
    in_specs = (P(None, None, "gx", "gy"), P("gx", "gy"), P("gx", "gy"), P(), P(), P(), P(), P())
    out_specs = (P(None, None, "gx", "gy"), P())
    return jax.shard_map(
        functools.partial(body, gx, gy), mesh=mesh, in_specs=in_specs, out_specs=out_specs, check_vma=False
    )
```

```python
import functools
import math

import jax
import jax.numpy as jnp
import numpy as np
from jax import lax
from jax.experimental import pallas as pl
from jax.experimental.pallas import tpu as pltpu
from jax.sharding import PartitionSpec as P

MESH = pl.DeviceIdType.MESH
OFFSETS = ((1, 0), (0, 1), (1, 1), (1, -1), (2, 0), (0, 2))
F32 = jnp.float32
BF16 = jnp.bfloat16
COUNT, PARTS, ROWS, LANES = 64, 6, 8, 128
PIECES = 8
PANEL = 4
AHEAD = 2
GRAM_GROUP = 1
GROUPS = 4
PER = COUNT // GROUPS
BATCH = 8
STEPS = (-1, 0, 1, 2)
NODE_ROWS = PARTS * ROWS


def halo_row(step_y, x):
    return {0: {8: 0, 9: 1, -2: 6, -1: 7}, 1: {8: 3, -1: 2}, -1: {8: 5, -1: 4}}[step_y][x]


DEPTH = (len(STEPS) + 1) * NODE_ROWS


def stencil_masks():
    n = len(OFFSETS)
    out = np.zeros((2 * n, ROWS, DEPTH), np.float32)
    for i, sign in enumerate((1, -1)):
        for q, (ox, oy) in enumerate(OFFSETS):
            dx, dy = sign * ox, sign * oy
            for x in range(ROWS):
                for d in range(PARTS):
                    if dy not in STEPS:
                        continue
                    if 0 <= x + dx < ROWS:
                        at = STEPS.index(dy) * NODE_ROWS + d * ROWS + x + dx
                    else:
                        at = len(STEPS) * NODE_ROWS + d * ROWS + halo_row(dy, x + dx)
                    out[i * n + q, x, at] = 1.0
    return out


def spread():
    out = np.zeros((PARTS, DEPTH), np.float32)
    for at in range(DEPTH):
        out[(at % NODE_ROWS) // ROWS, at] = 1.0
    return out


def split(x):
    hi = x.astype(BF16)
    return hi, (x - hi.astype(F32)).astype(BF16)


def build(coup_ref, spread_ref, mask_ref, both, out_ref):
    n = len(OFFSETS)
    expand = spread_ref[...]
    rows, beside = [None] * PARTS, []
    for s in range(2 * n - 1 if both else n):
        dims = (((1 if s < n else 0,), (0,)), ((), ()))
        wide = lax.dot_general(
            coup_ref[s % n], expand, dims, precision=lax.Precision.HIGHEST, preferred_element_type=F32
        )
        for c in range(PARTS):
            term = wide[c : c + 1, :] * mask_ref[s]
            rows[c] = term if rows[c] is None else rows[c] + term
    near = mask_ref[0] + mask_ref[n] if both else mask_ref[0]
    for c in range(PARTS):
        beside.append(expand[c : c + 1, :] * near)
    hi, lo = split(jnp.concatenate(rows, axis=0))
    out_ref[0:NODE_ROWS] = hi
    out_ref[NODE_ROWS : 2 * NODE_ROWS] = jnp.concatenate(beside, axis=0).astype(BF16)
    out_ref[2 * NODE_ROWS :] = lo


def stencil_kernel(
    gx, gy,
    dir_hbm, scale_hbm, mask_hbm, srow_hbm, scol_hbm, center_hbm, coup_hbm, stiff_hbm,
    masks_hbm, spread_hbm,
    basis_out, projected_ref,
    dir_ref, scale_ref, mask_ref, srow_ref, scol_ref, center_ref, coup_ref, stiff_ref,
    masks_ref, spread_ref, in_sems, dir_sems,
    u, hx, prod, u2, hx2, image,
    pk, pyp, pym, hcp, hcm, pk2, py2p, py2m, hc2p, hc2m,
    m1, m2, far_coup, flat, iflat, g_own, g_a, g_b, c_own, c_a, c_b, basis,
    xs_send, xs_recv, ys_send, ys_recv, cs_send, cs_recv,
    ga_send, ga_recv, gb_send, gb_recv, ca_send, ca_recv, cb_send, cb_recv, out_sem,
):
    small = [
        pltpu.make_async_copy(src, dst, in_sems.at[i])
        for i, (src, dst) in enumerate((
            (scale_hbm, scale_ref), (mask_hbm, mask_ref), (srow_hbm, srow_ref), (scol_hbm, scol_ref),
            (center_hbm, center_ref), (coup_hbm, coup_ref), (stiff_hbm, stiff_ref), (masks_hbm, masks_ref),
            (spread_hbm, spread_ref),
        ))
    ]
    large = []
    for i in range(GROUPS):
        part = pl.ds(i * PER * PARTS, PER * PARTS)
        large.append(pltpu.make_async_copy(dir_hbm.at[part], dir_ref.at[part], dir_sems.at[i]))
    for copy in small[:2] + large + small[2:]:
        copy.start()
    ix, iy = lax.axis_index("gx"), lax.axis_index("gy")
    xp, xm = lax.rem(ix + 1, gx), lax.rem(ix + gx - 1, gx)
    yp, ym = lax.rem(iy + 1, gy), lax.rem(iy + gy - 1, gy)

    barrier = pltpu.get_barrier_semaphore()

    def greet(px, py):
        pl.semaphore_signal(barrier, inc=1, device_id=(px, py), device_id_type=MESH)

    na, nb = gx // 2, 2 * gy
    ia, ib = lax.rem(ix, na), lax.div(ix, na) * gy + iy

    def peer_a(j):
        return lax.div(ix, na) * na + lax.rem(ia + j, na), iy

    def peer_b(j):
        to = lax.rem(ib + j, nb)
        return lax.div(to, gy) * na + ia, lax.rem(to, gy)

    for j in range(1, na):
        greet(*peer_a(j))
    for j in range(1, nb):
        greet(*peer_b(j))
    for px in (xp, xm):
        greet(px, iy)
        for py in (yp, ym):
            greet(px, py)
    for py in (yp, ym):
        greet(ix, py)

    lane = lax.broadcasted_iota(jnp.int32, (ROWS, LANES), 1)
    row = lax.broadcasted_iota(jnp.int32, (ROWS, LANES), 0)
    small[0].wait()
    small[1].wait()
    mask = mask_ref[...].astype(F32)
    weight = scale_ref[...] * (1.0 - mask)

    def scale_body(i, _):
        g = lax.div(i, PER // BATCH)
        m = lax.rem(i, PER // BATCH) * BATCH
        for c in range(PARTS):
            packed = pk[g * PARTS + c]
            for b in range(BATCH):
                at = (i * BATCH + b) * PARTS + c
                value = weight * dir_ref[at]
                u[at] = value
                moved = pltpu.roll(value, lax.rem(4 * (m + b) + 2, LANES), 1)
                packed = jnp.where(lax.div(lane, 4) == m + b, moved, packed)
            pk[g * PARTS + c] = packed
        return 0

    pk[...] = jnp.zeros_like(pk)

    def remote(src, dst, send, recv, px, py):
        return pltpu.make_async_remote_copy(
            src_ref=src, dst_ref=dst, send_sem=send, recv_sem=recv,
            device_id=(px, py), device_id_type=MESH,
        )

    def x_copies(src, dst, g, base, down):
        part = pl.ds(g * PER * PARTS, PER * PARTS)
        top = pl.ds(0, 2)
        out = [remote(src.at[part, top], dst.at[part, top], xs_send.at[base], xs_recv.at[base], xm, iy)]
        if down:
            low = pl.ds(6, 2)
            out.append(
                remote(src.at[part, low], dst.at[part, low], xs_send.at[base + 1], xs_recv.at[base + 1], xp, iy)
            )
        return out

    def y_copies(src, dst_p, dst_m, cp, cm, part, base, down):
        first = pl.ds(0, 1)
        last = pl.ds(7, 1)
        out = [
            remote(src.at[part], dst_p.at[part], ys_send.at[base], ys_recv.at[base], ix, ym),
            remote(src.at[part], dst_m.at[part], ys_send.at[base + 1], ys_recv.at[base + 1], ix, yp),
        ]
        k = 2 * base
        out.append(remote(src.at[part, first], cp.at[part, first], cs_send.at[k], cs_recv.at[k], xm, ym))
        out.append(remote(src.at[part, first], cm.at[part, first], cs_send.at[k + 1], cs_recv.at[k + 1], xm, yp))
        if down:
            out.append(remote(src.at[part, last], cp.at[part, last], cs_send.at[k + 2], cs_recv.at[k + 2], xp, ym))
            out.append(remote(src.at[part, last], cm.at[part, last], cs_send.at[k + 3], cs_recv.at[k + 3], xp, yp))
        return out

    firsts = []
    for g in range(GROUPS):
        large[g].wait()
        lax.fori_loop(g * PER // BATCH, (g + 1) * PER // BATCH, scale_body, 0)
        if g == 0:
            pl.semaphore_wait(barrier, (na - 1) + (nb - 1) + 8)
        copies = y_copies(pk, pyp, pym, hcp, hcm, pl.ds(g * PARTS, PARTS), 2 * g, True)
        copies += x_copies(u, hx, g, 2 * g, True)
        if g >= AHEAD:
            for copy in firsts[g - AHEAD]:
                copy.wait_send()
        for copy in copies:
            copy.start()
        firsts.append(copies)

    for copy in small[2:]:
        copy.wait()

    rows_hit = jnp.zeros((ROWS, LANES), F32)
    for f in range(srow_ref.shape[0]):
        rows_hit = rows_hit + (row + ix * ROWS == srow_ref[f]).astype(F32)
    cols_hit = jnp.zeros((ROWS, LANES), F32)
    for f in range(scol_ref.shape[0]):
        cols_hit = cols_hit + (lane + iy * LANES == scol_ref[f]).astype(F32)
    build(coup_ref, spread_ref, masks_ref, True, m1)
    build(coup_ref, spread_ref, masks_ref, False, m2)
    last = coup_ref[len(OFFSETS) - 1]
    for c in range(PARTS):
        for d in range(PARTS):
            far_coup[c * PARTS + d] = jnp.broadcast_to(last[d : d + 1, c : c + 1], (ROWS, LANES))

    zero = jnp.zeros((ROWS, LANES), F32)
    from_minus = lax.rem(lane, 4) < 2
    in_xp = jnp.full((ROWS, LANES), ix, jnp.int32) < gx - 1
    in_xm = jnp.full((ROWS, LANES), ix, jnp.int32) > 0
    in_yp = jnp.full((ROWS, LANES), iy, jnp.int32) < gy - 1
    in_ym = jnp.full((ROWS, LANES), iy, jnp.int32) > 0
    in_x = (in_xp & (row < 4)) | (in_xm & (row >= 4))
    in_x2 = in_xp & (row < 2)
    in_y = (in_ym & from_minus) | (in_yp & (lax.rem(lane, 4) >= 2))

    def merge_y(minus, plus, cminus, cplus, n, start, in_corner):
        for i in range(n):
            at = start + i
            plus[at] = jnp.where(in_y, jnp.where(from_minus, minus[at], plus[at]), zero)
            cplus[at] = jnp.where(in_y & in_corner, jnp.where(from_minus, cminus[at], cplus[at]), zero)

    def windows(source, hx_ref, py_ref, hc_ref, k, g, m, inside, both):
        back = LANES - 2 - 4 * m
        tiles = {s: [] for s in STEPS}
        halo, far = [], []
        for d in range(PARTS):
            at = k * PARTS + d
            v = source[at]
            h = jnp.where(inside, hx_ref[at], zero)
            hy = pltpu.roll(py_ref[g * PARTS + d], back, 1)
            hc = pltpu.roll(hc_ref[g * PARTS + d], back, 1)
            for s in STEPS:
                if s == 0:
                    tiles[s].append(v)
                elif s > 0:
                    tiles[s].append(pltpu.roll(jnp.where(lane < s, hy, v), LANES - s, 1))
                else:
                    tiles[s].append(pltpu.roll(jnp.where(lane >= LANES + s, hy, v), -s, 1))
            if both:
                far.append(pltpu.roll(jnp.where(lane >= LANES - 2, hy, v), 2, 1))
            right = pltpu.roll(jnp.where(lane < 1, hc, h), LANES - 1, 1)
            left = pltpu.roll(jnp.where(lane >= LANES - 1, hc, h), 1, 1)
            right = pltpu.roll(right, 3, 0)
            left = pltpu.roll(left, 5, 0)
            halo.append(jnp.where((row == 2) | (row == 3), right, jnp.where((row == 4) | (row == 5), left, h)))
        stack = jnp.concatenate([t for s in STEPS for t in tiles[s]] + halo, axis=0)
        return stack, tiles, far

    def couple(stacks, m_ref):
        hi, lo = split(jnp.concatenate(stacks, axis=1))
        top = jnp.dot(m_ref[...], hi, preferred_element_type=F32)
        low = jnp.dot(m_ref[0 : 2 * NODE_ROWS], lo, preferred_element_type=F32)
        return top[0:NODE_ROWS] + (top[2 * NODE_ROWS :] + low[0:NODE_ROWS]), (
            top[NODE_ROWS : 2 * NODE_ROWS] + low[NODE_ROWS:]
        )

    def tile_of(x, c, b):
        return x[c * ROWS : (c + 1) * ROWS, b * LANES : (b + 1) * LANES]

    def apply_body(g, i, _):
        m = i * BATCH
        first = g * PER + m
        got = [windows(u, hx, pyp, hcp, first + b, g, m + b, in_x, True) for b in range(BATCH)]
        total, beside = couple([w[0] for w in got], m1)
        for c in range(PARTS):
            packed = pk2[g * PARTS + c]
            frame = stiff_ref[0, c] * rows_hit
            stringer = stiff_ref[1, c] * cols_hit
            local = center_ref[c] + 2.0 * frame + 2.0 * stringer
            for b in range(BATCH):
                _, tiles, far = got[b]
                v = tile_of(total, c, b) + local * tiles[0][c]
                v = v - frame * (tiles[1][c] + tiles[-1][c]) - stringer * tile_of(beside, c, b)
                for d in range(PARTS):
                    v = v + far_coup[c * PARTS + d] * far[d]
                at = (first + b) * PARTS + c
                value = weight * v + mask * dir_ref[at]
                prod[pl.ds(pl.multiple_of(at * ROWS, ROWS), ROWS), :] = value
                scaled = weight * value
                u2[at] = scaled
                moved = pltpu.roll(scaled, lax.rem(4 * (m + b) + 2, LANES), 1)
                packed = jnp.where(lax.div(lane, 4) == m + b, moved, packed)
            pk2[g * PARTS + c] = packed
        return 0

    pk2[...] = jnp.zeros_like(pk2)
    second = []
    for g in range(GROUPS):
        for copy in firsts[g]:
            copy.wait_recv()
        merge_y(pym, pyp, hcm, hcp, PARTS, g * PARTS, in_x)
        lax.fori_loop(0, PER // BATCH, functools.partial(apply_body, g), 0)
        x2 = x_copies(u2, hx2, g, 2 * GROUPS + g, False)
        y2 = y_copies(pk2, py2p, py2m, hc2p, hc2m, pl.ds(g * PARTS, PARTS), 2 * GROUPS + 2 * g, False)
        for copy in y2 + x2:
            copy.start()
        second.append(y2 + x2)

    def send_all(own, slots, mine, peer, count, send, recv):
        copies = []
        for j in range(1, count):
            copies.append(remote(own, slots.at[mine], send.at[j], recv.at[j], *peer(j)))
        for copy in copies:
            copy.start()
        return copies

    def receive_sum(copies, own, slots, mine, count):
        slots[mine] = own[...]
        for copy in copies:
            copy.wait_recv()
        total = slots[0]
        for j in range(1, count):
            total = total + slots[j]
        return total

    def regroup(source, target):
        for at in range(NODE_ROWS):
            hi, lo = split(source[pl.ds(at, COUNT, stride=NODE_ROWS), :])
            target[0:COUNT, at * LANES : (at + 1) * LANES] = hi
            target[COUNT : 2 * COUNT, at * LANES : (at + 1) * LANES] = lo

    def inner(left, right):
        big = lax.dot_general(left[...], right[...], (((1,), (1,)), ((), ())), preferred_element_type=F32)
        fold = big[0:COUNT] + big[COUNT : 2 * COUNT]
        fold = fold[:, 0:COUNT] + fold[:, COUNT : 2 * COUNT]
        return jnp.concatenate([fold[0 : COUNT // 2], fold[COUNT // 2 :]], axis=1)

    def unfold(x):
        return jnp.concatenate([x[:, 0:COUNT], x[:, COUNT : 2 * COUNT]], axis=0)

    regroup(prod, flat)
    g_own[0] = inner(flat, flat)
    g_first = send_all(g_own.at[0], g_a, ia, peer_a, na, ga_send, ga_recv)

    def image_body(g, i, _):
        m = i * BATCH
        first = g * PER + m
        got = [windows(u2, hx2, py2p, hc2p, first + b, g, m + b, in_x2, False) for b in range(BATCH)]
        total, beside = couple([w[0] for w in got], m2)
        for c in range(PARTS):
            frame = stiff_ref[0, c] * rows_hit
            stringer = stiff_ref[1, c] * cols_hit
            local = 0.5 * center_ref[c] + frame + stringer
            for b in range(BATCH):
                _, tiles, _ = got[b]
                v = tile_of(total, c, b) + local * tiles[0][c]
                v = v - frame * tiles[1][c] - stringer * tile_of(beside, c, b)
                at = pl.ds(pl.multiple_of(((first + b) * PARTS + c) * ROWS, ROWS), ROWS)
                image[at, :] = weight * v + (0.5 * mask) * prod[at, :]
        return 0

    for g in range(GROUPS):
        for copy in second[g]:
            copy.wait_recv()
        merge_y(py2m, py2p, hc2m, hc2p, PARTS, g * PARTS, in_x2)
        lax.fori_loop(0, PER // BATCH, functools.partial(image_body, g), 0)
        if g == GRAM_GROUP:
            g_own[1] = receive_sum(g_first, g_own.at[0], g_a, ia, na)
            g_second = send_all(g_own.at[1], g_b, ib, peer_b, nb, gb_send, gb_recv)
    regroup(image, iflat)
    c_own[0] = inner(flat, iflat)
    c_first = send_all(c_own.at[0], c_a, ia, peer_a, na, ca_send, ca_recv)

    c_own[1] = receive_sum(c_first, c_own.at[0], c_a, ia, na)
    c_second = send_all(c_own.at[1], c_b, ib, peer_b, nb, cb_send, cb_recv)
    gram = unfold(receive_sum(g_second, g_own.at[1], g_b, ib, nb))
    tiles = []
    for i in range(COUNT // ROWS):
        unit = (lax.broadcasted_iota(jnp.int32, (ROWS, COUNT), 1) == i * ROWS
                + lax.broadcasted_iota(jnp.int32, (ROWS, COUNT), 0)).astype(F32)
        tiles.append(jnp.concatenate([gram[i * ROWS : (i + 1) * ROWS], unit], axis=1))
    for first in range(0, COUNT, PANEL):
        block, inside = first // ROWS, first % ROWS
        here = range(block, COUNT // ROWS)
        cols = [{i: jnp.broadcast_to(tiles[i][:, first + j : first + j + 1], (ROWS, LANES)) for i in here}
                for j in range(PANEL)]
        lines = [tiles[block][inside + j : inside + j + 1, :] for j in range(PANEL)]
        for a in range(PANEL):
            at = inside + a
            over = 1.0 / cols[a][block][at : at + 1, :]
            line = lines[a] * over
            for j in range(a + 1, PANEL):
                ratio = cols[j][block][at : at + 1, :] * over
                lines[j] = lines[j] - cols[a][block][inside + j : inside + j + 1, :] * line
                for i in here:
                    cols[j][i] = cols[j][i] - cols[a][i] * ratio
            for i in here:
                col = jnp.where(row > at, cols[a][i], 0.0) if i == block else cols[a][i]
                tiles[i] = tiles[i] - col * line
    for i in range(COUNT // ROWS):
        pivots = jnp.sum(jnp.where(lane == row + i * ROWS, tiles[i], 0.0), axis=1, keepdims=True)
        tiles[i] = tiles[i] * lax.rsqrt(pivots)
    inverse_t = jnp.concatenate(tiles, axis=0)[:, COUNT : 2 * COUNT]

    scale = math.sqrt(PARTS * gx * ROWS * gy * LANES)
    hi, lo = split(scale * inverse_t)
    factors = jnp.concatenate([hi, hi, lo], axis=1)
    width = 2 * LANES
    for i in range(NODE_ROWS // 2):
        cols = slice(i * width, (i + 1) * width)
        fields = jnp.concatenate([flat[:, cols], flat[0:COUNT, cols]], axis=0)
        value = jnp.dot(factors, fields, preferred_element_type=F32)
        for j in range(2):
            basis[pl.ds(2 * i + j, COUNT, stride=NODE_ROWS), :] = value[:, j * LANES : (j + 1) * LANES]
    keep = pltpu.make_async_copy(basis, basis_out, out_sem)
    keep.start()

    half = unfold(receive_sum(c_second, c_own.at[1], c_b, ib, nb))
    cross = half + half.T
    left = jnp.dot(inverse_t, cross, precision=lax.Precision.HIGHEST, preferred_element_type=F32)
    projected_ref[...] = lax.dot_general(
        left, inverse_t, (((1,), (1,)), ((), ())), precision=lax.Precision.HIGHEST, preferred_element_type=F32
    )
    for copy in [c for g in firsts[-AHEAD:] + second for c in g]:
        copy.wait_send()
    for copy in g_first + g_second + c_first + c_second:
        copy.wait_send()
    keep.wait()


def hand_over_kernel(basis_in, projected_in, basis_out, projected_out, basis, projected, in_sems, out_sems):
    rows = basis_in.shape[0] // PIECES
    ways = [(basis_in.at[part], basis.at[part], basis_out.at[part])
            for part in (pl.ds(i * rows, rows) for i in range(PIECES))]
    ways.append((projected_in, projected, projected_out))
    arrive = [pltpu.make_async_copy(a, b, in_sems.at[i]) for i, (a, b, _) in enumerate(ways)]
    leave = [pltpu.make_async_copy(b, c, out_sems.at[i]) for i, (_, b, c) in enumerate(ways)]
    for copy in arrive:
        copy.start()
    for first, then in zip(arrive, leave):
        first.wait()
        then.start()
    for copy in leave:
        copy.wait()


def body(gx, gy, directions, node_scale, boundary_mask, stiffener_rows, stiffener_cols, center, couplings, stiffness):
    tiles = COUNT * PARTS
    nodes = NODE_ROWS * LANES
    na, nb = gx // 2, 2 * gy
    vmem = pl.BlockSpec(memory_space=pltpu.VMEM)
    hbm = pl.BlockSpec(memory_space=pl.ANY)
    field = pltpu.VMEM((tiles, ROWS, LANES), F32)
    plain = pltpu.VMEM((tiles * ROWS, LANES), F32)
    edge = pltpu.VMEM((GROUPS * PARTS, ROWS, LANES), F32)
    parts = pltpu.VMEM((2 * COUNT, nodes), BF16)
    matrix = pltpu.VMEM((3 * NODE_ROWS, DEPTH), BF16)
    small = (COUNT // 2, 2 * COUNT)
    dma = pltpu.SemaphoreType.DMA
    basis, projected = pl.pallas_call(
        functools.partial(stencil_kernel, gx, gy),
        out_shape=(
            jax.ShapeDtypeStruct((tiles * ROWS, LANES), F32),
            jax.ShapeDtypeStruct((COUNT, COUNT), F32),
        ),
        in_specs=[hbm] * 10,
        out_specs=(hbm, vmem),
        scratch_shapes=[
            field, pltpu.VMEM((ROWS, LANES), F32), pltpu.VMEM((ROWS, LANES), jnp.int32),
            pltpu.SMEM(stiffener_rows.shape, jnp.int32), pltpu.SMEM(stiffener_cols.shape, jnp.int32),
            pltpu.SMEM((PARTS,), F32), pltpu.VMEM((len(OFFSETS), PARTS, PARTS), F32), pltpu.SMEM((2, PARTS), F32),
            pltpu.VMEM((2 * len(OFFSETS), ROWS, DEPTH), F32), pltpu.VMEM((PARTS, DEPTH), F32),
            dma((9,)), dma((GROUPS,)),
            field, field, plain, field, field, plain,
            edge, edge, edge, edge, edge, edge, edge, edge, edge, edge,
            matrix, matrix, pltpu.VMEM((PARTS * PARTS, ROWS, LANES), F32), parts, parts,
            pltpu.VMEM((2,) + small, F32), pltpu.VMEM((na,) + small, F32), pltpu.VMEM((nb,) + small, F32),
            pltpu.VMEM((2,) + small, F32), pltpu.VMEM((na,) + small, F32), pltpu.VMEM((nb,) + small, F32),
            plain,
            dma((3 * GROUPS,)), dma((3 * GROUPS,)),
            dma((4 * GROUPS,)), dma((4 * GROUPS,)),
            dma((8 * GROUPS,)), dma((8 * GROUPS,)),
            dma((na,)), dma((na,)), dma((nb,)), dma((nb,)),
            dma((na,)), dma((na,)), dma((nb,)), dma((nb,)),
            dma(()),
        ],
        compiler_params=pltpu.CompilerParams(
            collective_id=0, has_side_effects=True, vmem_limit_bytes=63 * 1024 * 1024
        ),
        name="stencil",
    )(
        directions.reshape(tiles, ROWS, LANES), node_scale, boundary_mask, stiffener_rows, stiffener_cols,
        center, couplings, stiffness, jnp.asarray(stencil_masks()), jnp.asarray(spread()),
    )
    basis, projected = pl.pallas_call(
        hand_over_kernel,
        out_shape=(
            jax.ShapeDtypeStruct((tiles * ROWS, LANES), F32),
            jax.ShapeDtypeStruct((COUNT, COUNT), F32),
        ),
        in_specs=[hbm, hbm],
        out_specs=(hbm, hbm),
        scratch_shapes=[plain, pltpu.VMEM((COUNT, COUNT), F32), dma((PIECES + 1,)), dma((PIECES + 1,))],
        compiler_params=pltpu.CompilerParams(vmem_limit_bytes=63 * 1024 * 1024),
        name="hand_over",
    )(basis, projected)
    return basis.reshape(COUNT, PARTS, ROWS, LANES), projected


def solution(mesh):
    gx, gy = mesh.shape["gx"], mesh.shape["gy"]
    in_specs = (P(None, None, "gx", "gy"), P("gx", "gy"), P("gx", "gy"), P(), P(), P(), P(), P())
    out_specs = (P(None, None, "gx", "gy"), P())
    return jax.shard_map(
        functools.partial(body, gx, gy), mesh=mesh, in_specs=in_specs, out_specs=out_specs, check_vma=False
    )
```

```python
import functools
import math

import jax
import jax.numpy as jnp
import numpy as np
from jax import lax
from jax.experimental import pallas as pl
from jax.experimental.pallas import tpu as pltpu
from jax.sharding import PartitionSpec as P

MESH = pl.DeviceIdType.MESH
OFFSETS = ((1, 0), (0, 1), (1, 1), (1, -1), (2, 0), (0, 2))
F32 = jnp.float32
BF16 = jnp.bfloat16
COUNT, PARTS, ROWS, LANES = 64, 6, 8, 128
PIECES = 4
PANEL = 4
AHEAD = 2
GRAM_GROUP = 3
GROUPS = 4
PER = COUNT // GROUPS
BATCH = 8
STEPS = (-1, 0, 1, 2)
NODE_ROWS = PARTS * ROWS


def halo_row(step_y, x):
    return {0: {8: 0, 9: 1, -2: 6, -1: 7}, 1: {8: 3, -1: 2}, -1: {8: 5, -1: 4}}[step_y][x]


DEPTH = (len(STEPS) + 1) * NODE_ROWS


def stencil_masks():
    n = len(OFFSETS)
    out = np.zeros((2 * n, ROWS, DEPTH), np.float32)
    for i, sign in enumerate((1, -1)):
        for q, (ox, oy) in enumerate(OFFSETS):
            dx, dy = sign * ox, sign * oy
            for x in range(ROWS):
                for d in range(PARTS):
                    if dy not in STEPS:
                        continue
                    if 0 <= x + dx < ROWS:
                        at = STEPS.index(dy) * NODE_ROWS + d * ROWS + x + dx
                    else:
                        at = len(STEPS) * NODE_ROWS + d * ROWS + halo_row(dy, x + dx)
                    out[i * n + q, x, at] = 1.0
    return out


def spread():
    out = np.zeros((PARTS, DEPTH), np.float32)
    for at in range(DEPTH):
        out[(at % NODE_ROWS) // ROWS, at] = 1.0
    return out


def split(x):
    hi = x.astype(BF16)
    return hi, (x - hi.astype(F32)).astype(BF16)


def build(coup_ref, spread_ref, mask_ref, both, out_ref):
    n = len(OFFSETS)
    expand = spread_ref[...]
    rows, beside = [None] * PARTS, []
    for s in range(2 * n - 1 if both else n):
        dims = (((1 if s < n else 0,), (0,)), ((), ()))
        wide = lax.dot_general(
            coup_ref[s % n], expand, dims, precision=lax.Precision.HIGHEST, preferred_element_type=F32
        )
        for c in range(PARTS):
            term = wide[c : c + 1, :] * mask_ref[s]
            rows[c] = term if rows[c] is None else rows[c] + term
    near = mask_ref[0] + mask_ref[n] if both else mask_ref[0]
    for c in range(PARTS):
        beside.append(expand[c : c + 1, :] * near)
    hi, lo = split(jnp.concatenate(rows, axis=0))
    out_ref[0:NODE_ROWS] = hi
    out_ref[NODE_ROWS : 2 * NODE_ROWS] = jnp.concatenate(beside, axis=0).astype(BF16)
    out_ref[2 * NODE_ROWS :] = lo


def stencil_kernel(
    gx, gy,
    dir_hbm, scale_hbm, mask_hbm, srow_hbm, scol_hbm, center_hbm, coup_hbm, stiff_hbm,
    masks_hbm, spread_hbm,
    basis_out, projected_ref,
    dir_ref, scale_ref, mask_ref, srow_ref, scol_ref, center_ref, coup_ref, stiff_ref,
    masks_ref, spread_ref, in_sems, dir_sems,
    u, hx, prod, u2, hx2, image,
    pk, pyp, pym, hcp, hcm, pk2, py2p, py2m, hc2p, hc2m,
    m1, m2, far_coup, flat, iflat, g_own, g_a, g_b, c_own, c_a, c_b, basis,
    xs_send, xs_recv, ys_send, ys_recv, cs_send, cs_recv,
    ga_send, ga_recv, gb_send, gb_recv, ca_send, ca_recv, cb_send, cb_recv, out_sem,
):
    small = [
        pltpu.make_async_copy(src, dst, in_sems.at[i])
        for i, (src, dst) in enumerate((
            (scale_hbm, scale_ref), (mask_hbm, mask_ref), (srow_hbm, srow_ref), (scol_hbm, scol_ref),
            (center_hbm, center_ref), (coup_hbm, coup_ref), (stiff_hbm, stiff_ref), (masks_hbm, masks_ref),
            (spread_hbm, spread_ref),
        ))
    ]
    large = []
    for i in range(GROUPS):
        part = pl.ds(i * PER * PARTS, PER * PARTS)
        large.append(pltpu.make_async_copy(dir_hbm.at[part], dir_ref.at[part], dir_sems.at[i]))
    for copy in small[:2] + large + small[2:]:
        copy.start()
    ix, iy = lax.axis_index("gx"), lax.axis_index("gy")
    xp, xm = lax.rem(ix + 1, gx), lax.rem(ix + gx - 1, gx)
    yp, ym = lax.rem(iy + 1, gy), lax.rem(iy + gy - 1, gy)

    barrier = pltpu.get_barrier_semaphore()

    def greet(px, py):
        pl.semaphore_signal(barrier, inc=1, device_id=(px, py), device_id_type=MESH)

    na, nb = gx // 2, 2 * gy
    ia, ib = lax.rem(ix, na), lax.div(ix, na) * gy + iy

    def peer_a(j):
        return lax.div(ix, na) * na + lax.rem(ia + j, na), iy

    def peer_b(j):
        to = lax.rem(ib + j, nb)
        return lax.div(to, gy) * na + ia, lax.rem(to, gy)

    for j in range(1, na):
        greet(*peer_a(j))
    for j in range(1, nb):
        greet(*peer_b(j))
    for px in (xp, xm):
        greet(px, iy)
        for py in (yp, ym):
            greet(px, py)
    for py in (yp, ym):
        greet(ix, py)

    lane = lax.broadcasted_iota(jnp.int32, (ROWS, LANES), 1)
    row = lax.broadcasted_iota(jnp.int32, (ROWS, LANES), 0)
    small[0].wait()
    small[1].wait()
    mask = mask_ref[...].astype(F32)
    weight = scale_ref[...] * (1.0 - mask)

    def scale_body(i, _):
        g = lax.div(i, PER // BATCH)
        m = lax.rem(i, PER // BATCH) * BATCH
        for c in range(PARTS):
            packed = pk[g * PARTS + c]
            for b in range(BATCH):
                at = (i * BATCH + b) * PARTS + c
                value = weight * dir_ref[at]
                u[at] = value
                moved = pltpu.roll(value, lax.rem(4 * (m + b) + 2, LANES), 1)
                packed = jnp.where(lax.div(lane, 4) == m + b, moved, packed)
            pk[g * PARTS + c] = packed
        return 0

    pk[...] = jnp.zeros_like(pk)

    def remote(src, dst, send, recv, px, py):
        return pltpu.make_async_remote_copy(
            src_ref=src, dst_ref=dst, send_sem=send, recv_sem=recv,
            device_id=(px, py), device_id_type=MESH,
        )

    def x_copies(src, dst, g, base, down):
        part = pl.ds(g * PER * PARTS, PER * PARTS)
        top = pl.ds(0, 2)
        out = [remote(src.at[part, top], dst.at[part, top], xs_send.at[base], xs_recv.at[base], xm, iy)]
        if down:
            low = pl.ds(6, 2)
            out.append(
                remote(src.at[part, low], dst.at[part, low], xs_send.at[base + 1], xs_recv.at[base + 1], xp, iy)
            )
        return out

    def y_copies(src, dst_p, dst_m, cp, cm, part, base, down):
        first = pl.ds(0, 1)
        last = pl.ds(7, 1)
        out = [
            remote(src.at[part], dst_p.at[part], ys_send.at[base], ys_recv.at[base], ix, ym),
            remote(src.at[part], dst_m.at[part], ys_send.at[base + 1], ys_recv.at[base + 1], ix, yp),
        ]
        k = 2 * base
        out.append(remote(src.at[part, first], cp.at[part, first], cs_send.at[k], cs_recv.at[k], xm, ym))
        out.append(remote(src.at[part, first], cm.at[part, first], cs_send.at[k + 1], cs_recv.at[k + 1], xm, yp))
        if down:
            out.append(remote(src.at[part, last], cp.at[part, last], cs_send.at[k + 2], cs_recv.at[k + 2], xp, ym))
            out.append(remote(src.at[part, last], cm.at[part, last], cs_send.at[k + 3], cs_recv.at[k + 3], xp, yp))
        return out

    firsts = []
    for g in range(GROUPS):
        large[g].wait()
        lax.fori_loop(g * PER // BATCH, (g + 1) * PER // BATCH, scale_body, 0)
        if g == 0:
            pl.semaphore_wait(barrier, (na - 1) + (nb - 1) + 8)
        copies = y_copies(pk, pyp, pym, hcp, hcm, pl.ds(g * PARTS, PARTS), 2 * g, True)
        copies += x_copies(u, hx, g, 2 * g, True)
        if g >= AHEAD:
            for copy in firsts[g - AHEAD]:
                copy.wait_send()
        for copy in copies:
            copy.start()
        firsts.append(copies)

    for copy in small[2:]:
        copy.wait()

    rows_hit = jnp.zeros((ROWS, LANES), F32)
    for f in range(srow_ref.shape[0]):
        rows_hit = rows_hit + (row + ix * ROWS == srow_ref[f]).astype(F32)
    cols_hit = jnp.zeros((ROWS, LANES), F32)
    for f in range(scol_ref.shape[0]):
        cols_hit = cols_hit + (lane + iy * LANES == scol_ref[f]).astype(F32)
    build(coup_ref, spread_ref, masks_ref, True, m1)
    build(coup_ref, spread_ref, masks_ref, False, m2)
    last = coup_ref[len(OFFSETS) - 1]
    for c in range(PARTS):
        for d in range(PARTS):
            far_coup[c * PARTS + d] = jnp.broadcast_to(last[d : d + 1, c : c + 1], (ROWS, LANES))

    zero = jnp.zeros((ROWS, LANES), F32)
    from_minus = lax.rem(lane, 4) < 2
    in_xp = jnp.full((ROWS, LANES), ix, jnp.int32) < gx - 1
    in_xm = jnp.full((ROWS, LANES), ix, jnp.int32) > 0
    in_yp = jnp.full((ROWS, LANES), iy, jnp.int32) < gy - 1
    in_ym = jnp.full((ROWS, LANES), iy, jnp.int32) > 0
    in_x = (in_xp & (row < 4)) | (in_xm & (row >= 4))
    in_x2 = in_xp & (row < 2)
    in_y = (in_ym & from_minus) | (in_yp & (lax.rem(lane, 4) >= 2))

    def merge_y(minus, plus, cminus, cplus, n, start, in_corner):
        for i in range(n):
            at = start + i
            plus[at] = jnp.where(in_y, jnp.where(from_minus, minus[at], plus[at]), zero)
            cplus[at] = jnp.where(in_y & in_corner, jnp.where(from_minus, cminus[at], cplus[at]), zero)

    def windows(source, hx_ref, py_ref, hc_ref, k, g, m, inside, both):
        back = LANES - 2 - 4 * m
        tiles = {s: [] for s in STEPS}
        halo, far = [], []
        for d in range(PARTS):
            at = k * PARTS + d
            v = source[at]
            h = jnp.where(inside, hx_ref[at], zero)
            hy = pltpu.roll(py_ref[g * PARTS + d], back, 1)
            hc = pltpu.roll(hc_ref[g * PARTS + d], back, 1)
            for s in STEPS:
                if s == 0:
                    tiles[s].append(v)
                elif s > 0:
                    tiles[s].append(pltpu.roll(jnp.where(lane < s, hy, v), LANES - s, 1))
                else:
                    tiles[s].append(pltpu.roll(jnp.where(lane >= LANES + s, hy, v), -s, 1))
            if both:
                far.append(pltpu.roll(jnp.where(lane >= LANES - 2, hy, v), 2, 1))
            right = pltpu.roll(jnp.where(lane < 1, hc, h), LANES - 1, 1)
            left = pltpu.roll(jnp.where(lane >= LANES - 1, hc, h), 1, 1)
            right = pltpu.roll(right, 3, 0)
            left = pltpu.roll(left, 5, 0)
            halo.append(jnp.where((row == 2) | (row == 3), right, jnp.where((row == 4) | (row == 5), left, h)))
        stack = jnp.concatenate([t for s in STEPS for t in tiles[s]] + halo, axis=0)
        return stack, tiles, far

    def couple(stacks, m_ref):
        hi, lo = split(jnp.concatenate(stacks, axis=1))
        top = jnp.dot(m_ref[...], hi, preferred_element_type=F32)
        low = jnp.dot(m_ref[0 : 2 * NODE_ROWS], lo, preferred_element_type=F32)
        return top[0:NODE_ROWS] + (top[2 * NODE_ROWS :] + low[0:NODE_ROWS]), (
            top[NODE_ROWS : 2 * NODE_ROWS] + low[NODE_ROWS:]
        )

    def tile_of(x, c, b):
        return x[c * ROWS : (c + 1) * ROWS, b * LANES : (b + 1) * LANES]

    def apply_body(g, i, _):
        m = i * BATCH
        first = g * PER + m
        got = [windows(u, hx, pyp, hcp, first + b, g, m + b, in_x, True) for b in range(BATCH)]
        total, beside = couple([w[0] for w in got], m1)
        for c in range(PARTS):
            packed = pk2[g * PARTS + c]
            frame = stiff_ref[0, c] * rows_hit
            stringer = stiff_ref[1, c] * cols_hit
            local = center_ref[c] + 2.0 * frame + 2.0 * stringer
            for b in range(BATCH):
                _, tiles, far = got[b]
                v = tile_of(total, c, b) + local * tiles[0][c]
                v = v - frame * (tiles[1][c] + tiles[-1][c]) - stringer * tile_of(beside, c, b)
                for d in range(PARTS):
                    v = v + far_coup[c * PARTS + d] * far[d]
                at = (first + b) * PARTS + c
                value = weight * v + mask * dir_ref[at]
                prod[pl.ds(pl.multiple_of(at * ROWS, ROWS), ROWS), :] = value
                scaled = weight * value
                u2[at] = scaled
                moved = pltpu.roll(scaled, lax.rem(4 * (m + b) + 2, LANES), 1)
                packed = jnp.where(lax.div(lane, 4) == m + b, moved, packed)
            pk2[g * PARTS + c] = packed
        return 0

    pk2[...] = jnp.zeros_like(pk2)
    second = []
    for g in range(GROUPS):
        for copy in firsts[g]:
            copy.wait_recv()
        merge_y(pym, pyp, hcm, hcp, PARTS, g * PARTS, in_x)
        lax.fori_loop(0, PER // BATCH, functools.partial(apply_body, g), 0)
        x2 = x_copies(u2, hx2, g, 2 * GROUPS + g, False)
        y2 = y_copies(pk2, py2p, py2m, hc2p, hc2m, pl.ds(g * PARTS, PARTS), 2 * GROUPS + 2 * g, False)
        for copy in y2 + x2:
            copy.start()
        second.append(y2 + x2)

    def send_all(own, slots, mine, peer, count, send, recv):
        copies = []
        for j in range(1, count):
            copies.append(remote(own, slots.at[mine], send.at[j], recv.at[j], *peer(j)))
        for copy in copies:
            copy.start()
        return copies

    def receive_sum(copies, own, slots, mine, count):
        slots[mine] = own[...]
        for copy in copies:
            copy.wait_recv()
        total = slots[0]
        for j in range(1, count):
            total = total + slots[j]
        return total

    def regroup(source, target):
        for at in range(NODE_ROWS):
            hi, lo = split(source[pl.ds(at, COUNT, stride=NODE_ROWS), :])
            target[0:COUNT, at * LANES : (at + 1) * LANES] = hi
            target[COUNT : 2 * COUNT, at * LANES : (at + 1) * LANES] = lo

    def inner(left, right):
        big = lax.dot_general(left[...], right[...], (((1,), (1,)), ((), ())), preferred_element_type=F32)
        fold = big[0:COUNT] + big[COUNT : 2 * COUNT]
        fold = fold[:, 0:COUNT] + fold[:, COUNT : 2 * COUNT]
        return jnp.concatenate([fold[0 : COUNT // 2], fold[COUNT // 2 :]], axis=1)

    def unfold(x):
        return jnp.concatenate([x[:, 0:COUNT], x[:, COUNT : 2 * COUNT]], axis=0)

    regroup(prod, flat)
    g_own[0] = inner(flat, flat)
    g_first = send_all(g_own.at[0], g_a, ia, peer_a, na, ga_send, ga_recv)

    def image_body(g, i, _):
        m = i * BATCH
        first = g * PER + m
        got = [windows(u2, hx2, py2p, hc2p, first + b, g, m + b, in_x2, False) for b in range(BATCH)]
        total, beside = couple([w[0] for w in got], m2)
        for c in range(PARTS):
            frame = stiff_ref[0, c] * rows_hit
            stringer = stiff_ref[1, c] * cols_hit
            local = 0.5 * center_ref[c] + frame + stringer
            for b in range(BATCH):
                _, tiles, _ = got[b]
                v = tile_of(total, c, b) + local * tiles[0][c]
                v = v - frame * tiles[1][c] - stringer * tile_of(beside, c, b)
                at = pl.ds(pl.multiple_of(((first + b) * PARTS + c) * ROWS, ROWS), ROWS)
                image[at, :] = weight * v + (0.5 * mask) * prod[at, :]
        return 0

    for g in range(GROUPS):
        for copy in second[g]:
            copy.wait_recv()
        merge_y(py2m, py2p, hc2m, hc2p, PARTS, g * PARTS, in_x2)
        lax.fori_loop(0, PER // BATCH, functools.partial(image_body, g), 0)
        if g == GRAM_GROUP:
            g_own[1] = receive_sum(g_first, g_own.at[0], g_a, ia, na)
            g_second = send_all(g_own.at[1], g_b, ib, peer_b, nb, gb_send, gb_recv)
    regroup(image, iflat)
    c_own[0] = inner(flat, iflat)
    c_first = send_all(c_own.at[0], c_a, ia, peer_a, na, ca_send, ca_recv)

    c_own[1] = receive_sum(c_first, c_own.at[0], c_a, ia, na)
    c_second = send_all(c_own.at[1], c_b, ib, peer_b, nb, cb_send, cb_recv)
    gram = unfold(receive_sum(g_second, g_own.at[1], g_b, ib, nb))
    tiles = []
    for i in range(COUNT // ROWS):
        unit = (lax.broadcasted_iota(jnp.int32, (ROWS, COUNT), 1) == i * ROWS
                + lax.broadcasted_iota(jnp.int32, (ROWS, COUNT), 0)).astype(F32)
        tiles.append(jnp.concatenate([gram[i * ROWS : (i + 1) * ROWS], unit], axis=1))
    for first in range(0, COUNT, PANEL):
        block, inside = first // ROWS, first % ROWS
        here = range(block, COUNT // ROWS)
        cols = [{i: jnp.broadcast_to(tiles[i][:, first + j : first + j + 1], (ROWS, LANES)) for i in here}
                for j in range(PANEL)]
        lines = [tiles[block][inside + j : inside + j + 1, :] for j in range(PANEL)]
        for a in range(PANEL):
            at = inside + a
            over = 1.0 / cols[a][block][at : at + 1, :]
            line = lines[a] * over
            for j in range(a + 1, PANEL):
                ratio = cols[j][block][at : at + 1, :] * over
                lines[j] = lines[j] - cols[a][block][inside + j : inside + j + 1, :] * line
                for i in here:
                    cols[j][i] = cols[j][i] - cols[a][i] * ratio
            for i in here:
                col = jnp.where(row > at, cols[a][i], 0.0) if i == block else cols[a][i]
                tiles[i] = tiles[i] - col * line
    for i in range(COUNT // ROWS):
        pivots = jnp.sum(jnp.where(lane == row + i * ROWS, tiles[i], 0.0), axis=1, keepdims=True)
        tiles[i] = tiles[i] * lax.rsqrt(pivots)
    inverse_t = jnp.concatenate(tiles, axis=0)[:, COUNT : 2 * COUNT]

    scale = math.sqrt(PARTS * gx * ROWS * gy * LANES)
    hi, lo = split(scale * inverse_t)
    factors = jnp.concatenate([hi, hi, lo], axis=1)
    width = 2 * LANES
    for i in range(NODE_ROWS // 2):
        cols = slice(i * width, (i + 1) * width)
        fields = jnp.concatenate([flat[:, cols], flat[0:COUNT, cols]], axis=0)
        value = jnp.dot(factors, fields, preferred_element_type=F32)
        for j in range(2):
            basis[pl.ds(2 * i + j, COUNT, stride=NODE_ROWS), :] = value[:, j * LANES : (j + 1) * LANES]
    keep = pltpu.make_async_copy(basis, basis_out, out_sem)
    keep.start()

    half = unfold(receive_sum(c_second, c_own.at[1], c_b, ib, nb))
    cross = half + half.T
    left = jnp.dot(inverse_t, cross, precision=lax.Precision.HIGHEST, preferred_element_type=F32)
    projected_ref[...] = lax.dot_general(
        left, inverse_t, (((1,), (1,)), ((), ())), precision=lax.Precision.HIGHEST, preferred_element_type=F32
    )
    for copy in [c for g in firsts[-AHEAD:] + second for c in g]:
        copy.wait_send()
    for copy in g_first + g_second + c_first + c_second:
        copy.wait_send()
    keep.wait()


def hand_over_kernel(basis_in, projected_in, basis_out, projected_out, basis, projected, in_sems, out_sems):
    rows = basis_in.shape[0] // PIECES
    ways = [(basis_in.at[part], basis.at[part], basis_out.at[part])
            for part in (pl.ds(i * rows, rows) for i in range(PIECES))]
    ways.append((projected_in, projected, projected_out))
    arrive = [pltpu.make_async_copy(a, b, in_sems.at[i]) for i, (a, b, _) in enumerate(ways)]
    leave = [pltpu.make_async_copy(b, c, out_sems.at[i]) for i, (_, b, c) in enumerate(ways)]
    for copy in arrive:
        copy.start()
    for first, then in zip(arrive, leave):
        first.wait()
        then.start()
    for copy in leave:
        copy.wait()


def body(gx, gy, directions, node_scale, boundary_mask, stiffener_rows, stiffener_cols, center, couplings, stiffness):
    tiles = COUNT * PARTS
    nodes = NODE_ROWS * LANES
    na, nb = gx // 2, 2 * gy
    vmem = pl.BlockSpec(memory_space=pltpu.VMEM)
    hbm = pl.BlockSpec(memory_space=pl.ANY)
    field = pltpu.VMEM((tiles, ROWS, LANES), F32)
    plain = pltpu.VMEM((tiles * ROWS, LANES), F32)
    edge = pltpu.VMEM((GROUPS * PARTS, ROWS, LANES), F32)
    parts = pltpu.VMEM((2 * COUNT, nodes), BF16)
    matrix = pltpu.VMEM((3 * NODE_ROWS, DEPTH), BF16)
    small = (COUNT // 2, 2 * COUNT)
    dma = pltpu.SemaphoreType.DMA
    basis, projected = pl.pallas_call(
        functools.partial(stencil_kernel, gx, gy),
        out_shape=(
            jax.ShapeDtypeStruct((tiles * ROWS, LANES), F32),
            jax.ShapeDtypeStruct((COUNT, COUNT), F32),
        ),
        in_specs=[hbm] * 10,
        out_specs=(hbm, vmem),
        scratch_shapes=[
            field, pltpu.VMEM((ROWS, LANES), F32), pltpu.VMEM((ROWS, LANES), jnp.int32),
            pltpu.SMEM(stiffener_rows.shape, jnp.int32), pltpu.SMEM(stiffener_cols.shape, jnp.int32),
            pltpu.SMEM((PARTS,), F32), pltpu.VMEM((len(OFFSETS), PARTS, PARTS), F32), pltpu.SMEM((2, PARTS), F32),
            pltpu.VMEM((2 * len(OFFSETS), ROWS, DEPTH), F32), pltpu.VMEM((PARTS, DEPTH), F32),
            dma((9,)), dma((GROUPS,)),
            field, field, plain, field, field, plain,
            edge, edge, edge, edge, edge, edge, edge, edge, edge, edge,
            matrix, matrix, pltpu.VMEM((PARTS * PARTS, ROWS, LANES), F32), parts, parts,
            pltpu.VMEM((2,) + small, F32), pltpu.VMEM((na,) + small, F32), pltpu.VMEM((nb,) + small, F32),
            pltpu.VMEM((2,) + small, F32), pltpu.VMEM((na,) + small, F32), pltpu.VMEM((nb,) + small, F32),
            plain,
            dma((3 * GROUPS,)), dma((3 * GROUPS,)),
            dma((4 * GROUPS,)), dma((4 * GROUPS,)),
            dma((8 * GROUPS,)), dma((8 * GROUPS,)),
            dma((na,)), dma((na,)), dma((nb,)), dma((nb,)),
            dma((na,)), dma((na,)), dma((nb,)), dma((nb,)),
            dma(()),
        ],
        compiler_params=pltpu.CompilerParams(
            collective_id=0, has_side_effects=True, vmem_limit_bytes=63 * 1024 * 1024
        ),
        name="stencil",
    )(
        directions.reshape(tiles, ROWS, LANES), node_scale, boundary_mask, stiffener_rows, stiffener_cols,
        center, couplings, stiffness, jnp.asarray(stencil_masks()), jnp.asarray(spread()),
    )
    basis, projected = pl.pallas_call(
        hand_over_kernel,
        out_shape=(
            jax.ShapeDtypeStruct((tiles * ROWS, LANES), F32),
            jax.ShapeDtypeStruct((COUNT, COUNT), F32),
        ),
        in_specs=[hbm, hbm],
        out_specs=(hbm, hbm),
        scratch_shapes=[plain, pltpu.VMEM((COUNT, COUNT), F32), dma((PIECES + 1,)), dma((PIECES + 1,))],
        compiler_params=pltpu.CompilerParams(vmem_limit_bytes=63 * 1024 * 1024),
        name="hand_over",
    )(basis, projected)
    return basis.reshape(COUNT, PARTS, ROWS, LANES), projected


def solution(mesh):
    gx, gy = mesh.shape["gx"], mesh.shape["gy"]
    in_specs = (P(None, None, "gx", "gy"), P("gx", "gy"), P("gx", "gy"), P(), P(), P(), P(), P())
    out_specs = (P(None, None, "gx", "gy"), P())
    return jax.shard_map(
        functools.partial(body, gx, gy), mesh=mesh, in_specs=in_specs, out_specs=out_specs, check_vma=False
    )
```

```python
import functools
import math

import jax
import jax.numpy as jnp
import numpy as np
from jax import lax
from jax.experimental import pallas as pl
from jax.experimental.pallas import tpu as pltpu
from jax.sharding import PartitionSpec as P

MESH = pl.DeviceIdType.MESH
OFFSETS = ((1, 0), (0, 1), (1, 1), (1, -1), (2, 0), (0, 2))
F32 = jnp.float32
BF16 = jnp.bfloat16
COUNT, PARTS, ROWS, LANES = 64, 6, 8, 128
PIECES = 4
PANEL = 4
AHEAD = 2
GRAM_GROUP = 3
GROUPS = 4
PER = COUNT // GROUPS
BATCH = 8
STEPS = (-1, 0, 1, 2)
NODE_ROWS = PARTS * ROWS


def halo_row(step_y, x):
    return {0: {8: 0, 9: 1, -2: 6, -1: 7}, 1: {8: 3, -1: 2}, -1: {8: 5, -1: 4}}[step_y][x]


DEPTH = (len(STEPS) + 1) * NODE_ROWS


def stencil_masks():
    n = len(OFFSETS)
    out = np.zeros((2 * n, ROWS, DEPTH), np.float32)
    for i, sign in enumerate((1, -1)):
        for q, (ox, oy) in enumerate(OFFSETS):
            dx, dy = sign * ox, sign * oy
            for x in range(ROWS):
                for d in range(PARTS):
                    if dy not in STEPS:
                        continue
                    if 0 <= x + dx < ROWS:
                        at = STEPS.index(dy) * NODE_ROWS + d * ROWS + x + dx
                    else:
                        at = len(STEPS) * NODE_ROWS + d * ROWS + halo_row(dy, x + dx)
                    out[i * n + q, x, at] = 1.0
    return out


def spread():
    out = np.zeros((PARTS, DEPTH), np.float32)
    for at in range(DEPTH):
        out[(at % NODE_ROWS) // ROWS, at] = 1.0
    return out


def split(x):
    hi = x.astype(BF16)
    return hi, (x - hi.astype(F32)).astype(BF16)


def build(coup_ref, spread_ref, mask_ref, both, out_ref):
    n = len(OFFSETS)
    expand = spread_ref[...]
    rows, beside = [None] * PARTS, []
    for s in range(2 * n - 1 if both else n):
        dims = (((1 if s < n else 0,), (0,)), ((), ()))
        wide = lax.dot_general(
            coup_ref[s % n], expand, dims, precision=lax.Precision.HIGHEST, preferred_element_type=F32
        )
        for c in range(PARTS):
            term = wide[c : c + 1, :] * mask_ref[s]
            rows[c] = term if rows[c] is None else rows[c] + term
    near = mask_ref[0] + mask_ref[n] if both else mask_ref[0]
    for c in range(PARTS):
        beside.append(expand[c : c + 1, :] * near)
    hi, lo = split(jnp.concatenate(rows, axis=0))
    out_ref[0:NODE_ROWS] = hi
    out_ref[NODE_ROWS : 2 * NODE_ROWS] = jnp.concatenate(beside, axis=0).astype(BF16)
    out_ref[2 * NODE_ROWS :] = lo


def stencil_kernel(
    gx, gy,
    dir_hbm, scale_hbm, mask_hbm, srow_hbm, scol_hbm, center_hbm, coup_hbm, stiff_hbm,
    masks_hbm, spread_hbm,
    basis_out, projected_ref,
    dir_ref, scale_ref, mask_ref, srow_ref, scol_ref, center_ref, coup_ref, stiff_ref,
    masks_ref, spread_ref, in_sems, dir_sems,
    u, hx, prod, u2, hx2, image,
    pk, pyp, pym, hcp, hcm, pk2, py2p, py2m, hc2p, hc2m,
    m1, m2, far_coup, flat, iflat, g_own, g_a, g_b, c_own, c_a, c_b, basis,
    xs_send, xs_recv, ys_send, ys_recv, cs_send, cs_recv,
    ga_send, ga_recv, gb_send, gb_recv, ca_send, ca_recv, cb_send, cb_recv, out_sem,
):
    small = [
        pltpu.make_async_copy(src, dst, in_sems.at[i])
        for i, (src, dst) in enumerate((
            (scale_hbm, scale_ref), (mask_hbm, mask_ref), (srow_hbm, srow_ref), (scol_hbm, scol_ref),
            (center_hbm, center_ref), (coup_hbm, coup_ref), (stiff_hbm, stiff_ref), (masks_hbm, masks_ref),
            (spread_hbm, spread_ref),
        ))
    ]
    large = []
    for i in range(GROUPS):
        part = pl.ds(i * PER * PARTS, PER * PARTS)
        large.append(pltpu.make_async_copy(dir_hbm.at[part], dir_ref.at[part], dir_sems.at[i]))
    for copy in small[:2] + large + small[2:]:
        copy.start()
    ix, iy = lax.axis_index("gx"), lax.axis_index("gy")
    xp, xm = lax.rem(ix + 1, gx), lax.rem(ix + gx - 1, gx)
    yp, ym = lax.rem(iy + 1, gy), lax.rem(iy + gy - 1, gy)

    barrier = pltpu.get_barrier_semaphore()

    def greet(px, py):
        pl.semaphore_signal(barrier, inc=1, device_id=(px, py), device_id_type=MESH)

    na, nb = gx // 2, 2 * gy
    ia, ib = lax.rem(ix, na), lax.div(ix, na) * gy + iy

    def peer_a(j):
        return lax.div(ix, na) * na + lax.rem(ia + j, na), iy

    def peer_b(j):
        to = lax.rem(ib + j, nb)
        return lax.div(to, gy) * na + ia, lax.rem(to, gy)

    for j in range(1, na):
        greet(*peer_a(j))
    for j in range(1, nb):
        greet(*peer_b(j))
    for px in (xp, xm):
        greet(px, iy)
        for py in (yp, ym):
            greet(px, py)
    for py in (yp, ym):
        greet(ix, py)

    lane = lax.broadcasted_iota(jnp.int32, (ROWS, LANES), 1)
    row = lax.broadcasted_iota(jnp.int32, (ROWS, LANES), 0)
    small[0].wait()
    small[1].wait()
    mask = mask_ref[...].astype(F32)
    weight = scale_ref[...] * (1.0 - mask)

    def scale_body(i, _):
        g = lax.div(i, PER // BATCH)
        m = lax.rem(i, PER // BATCH) * BATCH
        for c in range(PARTS):
            packed = pk[g * PARTS + c]
            for b in range(BATCH):
                at = (i * BATCH + b) * PARTS + c
                value = weight * dir_ref[at]
                u[at] = value
                moved = pltpu.roll(value, lax.rem(4 * (m + b) + 2, LANES), 1)
                packed = jnp.where(lax.div(lane, 4) == m + b, moved, packed)
            pk[g * PARTS + c] = packed
        return 0

    pk[...] = jnp.zeros_like(pk)

    def remote(src, dst, send, recv, px, py):
        return pltpu.make_async_remote_copy(
            src_ref=src, dst_ref=dst, send_sem=send, recv_sem=recv,
            device_id=(px, py), device_id_type=MESH,
        )

    def x_copies(src, dst, g, base, down):
        part = pl.ds(g * PER * PARTS, PER * PARTS)
        top = pl.ds(0, 2)
        out = [remote(src.at[part, top], dst.at[part, top], xs_send.at[base], xs_recv.at[base], xm, iy)]
        if down:
            low = pl.ds(6, 2)
            out.append(
                remote(src.at[part, low], dst.at[part, low], xs_send.at[base + 1], xs_recv.at[base + 1], xp, iy)
            )
        return out

    def y_copies(src, dst_p, dst_m, cp, cm, part, base, down):
        first = pl.ds(0, 1)
        last = pl.ds(7, 1)
        out = [
            remote(src.at[part], dst_p.at[part], ys_send.at[base], ys_recv.at[base], ix, ym),
            remote(src.at[part], dst_m.at[part], ys_send.at[base + 1], ys_recv.at[base + 1], ix, yp),
        ]
        k = 2 * base
        out.append(remote(src.at[part, first], cp.at[part, first], cs_send.at[k], cs_recv.at[k], xm, ym))
        out.append(remote(src.at[part, first], cm.at[part, first], cs_send.at[k + 1], cs_recv.at[k + 1], xm, yp))
        if down:
            out.append(remote(src.at[part, last], cp.at[part, last], cs_send.at[k + 2], cs_recv.at[k + 2], xp, ym))
            out.append(remote(src.at[part, last], cm.at[part, last], cs_send.at[k + 3], cs_recv.at[k + 3], xp, yp))
        return out

    firsts = []
    for g in range(GROUPS):
        large[g].wait()
        lax.fori_loop(g * PER // BATCH, (g + 1) * PER // BATCH, scale_body, 0)
        if g == 0:
            pl.semaphore_wait(barrier, (na - 1) + (nb - 1) + 8)
        copies = y_copies(pk, pyp, pym, hcp, hcm, pl.ds(g * PARTS, PARTS), 2 * g, True)
        copies += x_copies(u, hx, g, 2 * g, True)
        if g >= AHEAD:
            for copy in firsts[g - AHEAD]:
                copy.wait_send()
        for copy in copies[2:] + copies[:2]:
            copy.start()
        firsts.append(copies)

    for copy in small[2:]:
        copy.wait()

    rows_hit = jnp.zeros((ROWS, LANES), F32)
    for f in range(srow_ref.shape[0]):
        rows_hit = rows_hit + (row + ix * ROWS == srow_ref[f]).astype(F32)
    cols_hit = jnp.zeros((ROWS, LANES), F32)
    for f in range(scol_ref.shape[0]):
        cols_hit = cols_hit + (lane + iy * LANES == scol_ref[f]).astype(F32)
    build(coup_ref, spread_ref, masks_ref, True, m1)
    build(coup_ref, spread_ref, masks_ref, False, m2)
    last = coup_ref[len(OFFSETS) - 1]
    for c in range(PARTS):
        for d in range(PARTS):
            far_coup[c * PARTS + d] = jnp.broadcast_to(last[d : d + 1, c : c + 1], (ROWS, LANES))

    zero = jnp.zeros((ROWS, LANES), F32)
    from_minus = lax.rem(lane, 4) < 2
    in_xp = jnp.full((ROWS, LANES), ix, jnp.int32) < gx - 1
    in_xm = jnp.full((ROWS, LANES), ix, jnp.int32) > 0
    in_yp = jnp.full((ROWS, LANES), iy, jnp.int32) < gy - 1
    in_ym = jnp.full((ROWS, LANES), iy, jnp.int32) > 0
    in_x = (in_xp & (row < 4)) | (in_xm & (row >= 4))
    in_x2 = in_xp & (row < 2)
    in_y = (in_ym & from_minus) | (in_yp & (lax.rem(lane, 4) >= 2))

    def merge_y(minus, plus, cminus, cplus, n, start, in_corner):
        for i in range(n):
            at = start + i
            plus[at] = jnp.where(in_y, jnp.where(from_minus, minus[at], plus[at]), zero)
            cplus[at] = jnp.where(in_y & in_corner, jnp.where(from_minus, cminus[at], cplus[at]), zero)

    def windows(source, hx_ref, py_ref, hc_ref, k, g, m, inside, both):
        back = LANES - 2 - 4 * m
        tiles = {s: [] for s in STEPS}
        halo, far = [], []
        for d in range(PARTS):
            at = k * PARTS + d
            v = source[at]
            h = jnp.where(inside, hx_ref[at], zero)
            hy = pltpu.roll(py_ref[g * PARTS + d], back, 1)
            hc = pltpu.roll(hc_ref[g * PARTS + d], back, 1)
            for s in STEPS:
                if s == 0:
                    tiles[s].append(v)
                elif s > 0:
                    tiles[s].append(pltpu.roll(jnp.where(lane < s, hy, v), LANES - s, 1))
                else:
                    tiles[s].append(pltpu.roll(jnp.where(lane >= LANES + s, hy, v), -s, 1))
            if both:
                far.append(pltpu.roll(jnp.where(lane >= LANES - 2, hy, v), 2, 1))
            right = pltpu.roll(jnp.where(lane < 1, hc, h), LANES - 1, 1)
            left = pltpu.roll(jnp.where(lane >= LANES - 1, hc, h), 1, 1)
            right = pltpu.roll(right, 3, 0)
            left = pltpu.roll(left, 5, 0)
            halo.append(jnp.where((row == 2) | (row == 3), right, jnp.where((row == 4) | (row == 5), left, h)))
        stack = jnp.concatenate([t for s in STEPS for t in tiles[s]] + halo, axis=0)
        return stack, tiles, far

    def couple(stacks, m_ref):
        hi, lo = split(jnp.concatenate(stacks, axis=1))
        top = jnp.dot(m_ref[...], hi, preferred_element_type=F32)
        low = jnp.dot(m_ref[0 : 2 * NODE_ROWS], lo, preferred_element_type=F32)
        return top[0:NODE_ROWS] + (top[2 * NODE_ROWS :] + low[0:NODE_ROWS]), (
            top[NODE_ROWS : 2 * NODE_ROWS] + low[NODE_ROWS:]
        )

    def tile_of(x, c, b):
        return x[c * ROWS : (c + 1) * ROWS, b * LANES : (b + 1) * LANES]

    def apply_body(g, i, _):
        m = i * BATCH
        first = g * PER + m
        got = [windows(u, hx, pyp, hcp, first + b, g, m + b, in_x, True) for b in range(BATCH)]
        total, beside = couple([w[0] for w in got], m1)
        for c in range(PARTS):
            packed = pk2[g * PARTS + c]
            frame = stiff_ref[0, c] * rows_hit
            stringer = stiff_ref[1, c] * cols_hit
            local = center_ref[c] + 2.0 * frame + 2.0 * stringer
            for b in range(BATCH):
                _, tiles, far = got[b]
                v = tile_of(total, c, b) + local * tiles[0][c]
                v = v - frame * (tiles[1][c] + tiles[-1][c]) - stringer * tile_of(beside, c, b)
                for d in range(PARTS):
                    v = v + far_coup[c * PARTS + d] * far[d]
                at = (first + b) * PARTS + c
                value = weight * v + mask * dir_ref[at]
                prod[pl.ds(pl.multiple_of(at * ROWS, ROWS), ROWS), :] = value
                scaled = weight * value
                u2[at] = scaled
                moved = pltpu.roll(scaled, lax.rem(4 * (m + b) + 2, LANES), 1)
                packed = jnp.where(lax.div(lane, 4) == m + b, moved, packed)
            pk2[g * PARTS + c] = packed
        return 0

    pk2[...] = jnp.zeros_like(pk2)
    second = []
    for g in range(GROUPS):
        for copy in firsts[g]:
            copy.wait_recv()
        merge_y(pym, pyp, hcm, hcp, PARTS, g * PARTS, in_x)
        lax.fori_loop(0, PER // BATCH, functools.partial(apply_body, g), 0)
        x2 = x_copies(u2, hx2, g, 2 * GROUPS + g, False)
        y2 = y_copies(pk2, py2p, py2m, hc2p, hc2m, pl.ds(g * PARTS, PARTS), 2 * GROUPS + 2 * g, False)
        for copy in y2[2:] + x2 + y2[:2]:
            copy.start()
        second.append(y2 + x2)

    def send_all(own, slots, mine, peer, count, send, recv):
        copies = []
        for j in range(1, count):
            copies.append(remote(own, slots.at[mine], send.at[j], recv.at[j], *peer(j)))
        for copy in copies:
            copy.start()
        return copies

    def receive_sum(copies, own, slots, mine, count):
        slots[mine] = own[...]
        for copy in copies:
            copy.wait_recv()
        total = slots[0]
        for j in range(1, count):
            total = total + slots[j]
        return total

    def regroup(source, target):
        for at in range(NODE_ROWS):
            hi, lo = split(source[pl.ds(at, COUNT, stride=NODE_ROWS), :])
            target[0:COUNT, at * LANES : (at + 1) * LANES] = hi
            target[COUNT : 2 * COUNT, at * LANES : (at + 1) * LANES] = lo

    def inner(left, right):
        big = lax.dot_general(left[...], right[...], (((1,), (1,)), ((), ())), preferred_element_type=F32)
        fold = big[0:COUNT] + big[COUNT : 2 * COUNT]
        fold = fold[:, 0:COUNT] + fold[:, COUNT : 2 * COUNT]
        return jnp.concatenate([fold[0 : COUNT // 2], fold[COUNT // 2 :]], axis=1)

    def unfold(x):
        return jnp.concatenate([x[:, 0:COUNT], x[:, COUNT : 2 * COUNT]], axis=0)

    regroup(prod, flat)
    g_own[0] = inner(flat, flat)
    g_first = send_all(g_own.at[0], g_a, ia, peer_a, na, ga_send, ga_recv)

    def image_body(g, i, _):
        m = i * BATCH
        first = g * PER + m
        got = [windows(u2, hx2, py2p, hc2p, first + b, g, m + b, in_x2, False) for b in range(BATCH)]
        total, beside = couple([w[0] for w in got], m2)
        for c in range(PARTS):
            frame = stiff_ref[0, c] * rows_hit
            stringer = stiff_ref[1, c] * cols_hit
            local = 0.5 * center_ref[c] + frame + stringer
            for b in range(BATCH):
                _, tiles, _ = got[b]
                v = tile_of(total, c, b) + local * tiles[0][c]
                v = v - frame * tiles[1][c] - stringer * tile_of(beside, c, b)
                at = pl.ds(pl.multiple_of(((first + b) * PARTS + c) * ROWS, ROWS), ROWS)
                image[at, :] = weight * v + (0.5 * mask) * prod[at, :]
        return 0

    for g in range(GROUPS):
        for copy in second[g]:
            copy.wait_recv()
        merge_y(py2m, py2p, hc2m, hc2p, PARTS, g * PARTS, in_x2)
        lax.fori_loop(0, PER // BATCH, functools.partial(image_body, g), 0)
        if g == GRAM_GROUP:
            g_own[1] = receive_sum(g_first, g_own.at[0], g_a, ia, na)
            g_second = send_all(g_own.at[1], g_b, ib, peer_b, nb, gb_send, gb_recv)
    regroup(image, iflat)
    c_own[0] = inner(flat, iflat)
    c_first = send_all(c_own.at[0], c_a, ia, peer_a, na, ca_send, ca_recv)

    c_own[1] = receive_sum(c_first, c_own.at[0], c_a, ia, na)
    c_second = send_all(c_own.at[1], c_b, ib, peer_b, nb, cb_send, cb_recv)
    gram = unfold(receive_sum(g_second, g_own.at[1], g_b, ib, nb))
    tiles = []
    for i in range(COUNT // ROWS):
        unit = (lax.broadcasted_iota(jnp.int32, (ROWS, COUNT), 1) == i * ROWS
                + lax.broadcasted_iota(jnp.int32, (ROWS, COUNT), 0)).astype(F32)
        tiles.append(jnp.concatenate([gram[i * ROWS : (i + 1) * ROWS], unit], axis=1))
    for first in range(0, COUNT, PANEL):
        block, inside = first // ROWS, first % ROWS
        here = range(block, COUNT // ROWS)
        cols = [{i: jnp.broadcast_to(tiles[i][:, first + j : first + j + 1], (ROWS, LANES)) for i in here}
                for j in range(PANEL)]
        lines = [tiles[block][inside + j : inside + j + 1, :] for j in range(PANEL)]
        for a in range(PANEL):
            at = inside + a
            over = 1.0 / cols[a][block][at : at + 1, :]
            line = lines[a] * over
            for j in range(a + 1, PANEL):
                ratio = cols[j][block][at : at + 1, :] * over
                lines[j] = lines[j] - cols[a][block][inside + j : inside + j + 1, :] * line
                for i in here:
                    cols[j][i] = cols[j][i] - cols[a][i] * ratio
            for i in here:
                col = jnp.where(row > at, cols[a][i], 0.0) if i == block else cols[a][i]
                tiles[i] = tiles[i] - col * line
    for i in range(COUNT // ROWS):
        pivots = jnp.sum(jnp.where(lane == row + i * ROWS, tiles[i], 0.0), axis=1, keepdims=True)
        tiles[i] = tiles[i] * lax.rsqrt(pivots)
    inverse_t = jnp.concatenate(tiles, axis=0)[:, COUNT : 2 * COUNT]

    scale = math.sqrt(PARTS * gx * ROWS * gy * LANES)
    hi, lo = split(scale * inverse_t)
    factors = jnp.concatenate([hi, hi, lo], axis=1)
    width = 2 * LANES
    for i in range(NODE_ROWS // 2):
        cols = slice(i * width, (i + 1) * width)
        fields = jnp.concatenate([flat[:, cols], flat[0:COUNT, cols]], axis=0)
        value = jnp.dot(factors, fields, preferred_element_type=F32)
        for j in range(2):
            basis[pl.ds(2 * i + j, COUNT, stride=NODE_ROWS), :] = value[:, j * LANES : (j + 1) * LANES]
    keep = pltpu.make_async_copy(basis, basis_out, out_sem)
    keep.start()

    half = unfold(receive_sum(c_second, c_own.at[1], c_b, ib, nb))
    cross = half + half.T
    left = jnp.dot(inverse_t, cross, precision=lax.Precision.HIGHEST, preferred_element_type=F32)
    projected_ref[...] = lax.dot_general(
        left, inverse_t, (((1,), (1,)), ((), ())), precision=lax.Precision.HIGHEST, preferred_element_type=F32
    )
    for copy in [c for g in firsts[-AHEAD:] + second for c in g]:
        copy.wait_send()
    for copy in g_first + g_second + c_first + c_second:
        copy.wait_send()
    keep.wait()


def hand_over_kernel(basis_in, projected_in, basis_out, projected_out, basis, projected, in_sems, out_sems):
    rows = basis_in.shape[0] // PIECES
    ways = [(basis_in.at[part], basis.at[part], basis_out.at[part])
            for part in (pl.ds(i * rows, rows) for i in range(PIECES))]
    ways.append((projected_in, projected, projected_out))
    arrive = [pltpu.make_async_copy(a, b, in_sems.at[i]) for i, (a, b, _) in enumerate(ways)]
    leave = [pltpu.make_async_copy(b, c, out_sems.at[i]) for i, (_, b, c) in enumerate(ways)]
    for copy in arrive:
        copy.start()
    for first, then in zip(arrive, leave):
        first.wait()
        then.start()
    for copy in leave:
        copy.wait()


def body(gx, gy, directions, node_scale, boundary_mask, stiffener_rows, stiffener_cols, center, couplings, stiffness):
    tiles = COUNT * PARTS
    nodes = NODE_ROWS * LANES
    na, nb = gx // 2, 2 * gy
    vmem = pl.BlockSpec(memory_space=pltpu.VMEM)
    hbm = pl.BlockSpec(memory_space=pl.ANY)
    field = pltpu.VMEM((tiles, ROWS, LANES), F32)
    plain = pltpu.VMEM((tiles * ROWS, LANES), F32)
    edge = pltpu.VMEM((GROUPS * PARTS, ROWS, LANES), F32)
    parts = pltpu.VMEM((2 * COUNT, nodes), BF16)
    matrix = pltpu.VMEM((3 * NODE_ROWS, DEPTH), BF16)
    small = (COUNT // 2, 2 * COUNT)
    dma = pltpu.SemaphoreType.DMA
    basis, projected = pl.pallas_call(
        functools.partial(stencil_kernel, gx, gy),
        out_shape=(
            jax.ShapeDtypeStruct((tiles * ROWS, LANES), F32),
            jax.ShapeDtypeStruct((COUNT, COUNT), F32),
        ),
        in_specs=[hbm] * 10,
        out_specs=(hbm, vmem),
        scratch_shapes=[
            field, pltpu.VMEM((ROWS, LANES), F32), pltpu.VMEM((ROWS, LANES), jnp.int32),
            pltpu.SMEM(stiffener_rows.shape, jnp.int32), pltpu.SMEM(stiffener_cols.shape, jnp.int32),
            pltpu.SMEM((PARTS,), F32), pltpu.VMEM((len(OFFSETS), PARTS, PARTS), F32), pltpu.SMEM((2, PARTS), F32),
            pltpu.VMEM((2 * len(OFFSETS), ROWS, DEPTH), F32), pltpu.VMEM((PARTS, DEPTH), F32),
            dma((9,)), dma((GROUPS,)),
            field, field, plain, field, field, plain,
            edge, edge, edge, edge, edge, edge, edge, edge, edge, edge,
            matrix, matrix, pltpu.VMEM((PARTS * PARTS, ROWS, LANES), F32), parts, parts,
            pltpu.VMEM((2,) + small, F32), pltpu.VMEM((na,) + small, F32), pltpu.VMEM((nb,) + small, F32),
            pltpu.VMEM((2,) + small, F32), pltpu.VMEM((na,) + small, F32), pltpu.VMEM((nb,) + small, F32),
            plain,
            dma((3 * GROUPS,)), dma((3 * GROUPS,)),
            dma((4 * GROUPS,)), dma((4 * GROUPS,)),
            dma((8 * GROUPS,)), dma((8 * GROUPS,)),
            dma((na,)), dma((na,)), dma((nb,)), dma((nb,)),
            dma((na,)), dma((na,)), dma((nb,)), dma((nb,)),
            dma(()),
        ],
        compiler_params=pltpu.CompilerParams(
            collective_id=0, has_side_effects=True, vmem_limit_bytes=63 * 1024 * 1024
        ),
        name="stencil",
    )(
        directions.reshape(tiles, ROWS, LANES), node_scale, boundary_mask, stiffener_rows, stiffener_cols,
        center, couplings, stiffness, jnp.asarray(stencil_masks()), jnp.asarray(spread()),
    )
    basis, projected = pl.pallas_call(
        hand_over_kernel,
        out_shape=(
            jax.ShapeDtypeStruct((tiles * ROWS, LANES), F32),
            jax.ShapeDtypeStruct((COUNT, COUNT), F32),
        ),
        in_specs=[hbm, hbm],
        out_specs=(hbm, hbm),
        scratch_shapes=[plain, pltpu.VMEM((COUNT, COUNT), F32), dma((PIECES + 1,)), dma((PIECES + 1,))],
        compiler_params=pltpu.CompilerParams(vmem_limit_bytes=63 * 1024 * 1024),
        name="hand_over",
    )(basis, projected)
    return basis.reshape(COUNT, PARTS, ROWS, LANES), projected


def solution(mesh):
    gx, gy = mesh.shape["gx"], mesh.shape["gy"]
    in_specs = (P(None, None, "gx", "gy"), P("gx", "gy"), P("gx", "gy"), P(), P(), P(), P(), P())
    out_specs = (P(None, None, "gx", "gy"), P())
    return jax.shard_map(
        functools.partial(body, gx, gy), mesh=mesh, in_specs=in_specs, out_specs=out_specs, check_vma=False
    )
```
